128 devices in a mesh: blk: 16 (over y, z), ctr: 8 (over x, core).
Axes of the slice: x: 4, y: 4, z: 4, core: 2. Of those that a mesh axis runs over, the one named last changes fastest.
Arguments:
- three_centre: bfloat16 [8, 128, 3, 1024, 128], P('ctr', None, None, 'blk'), may hold values from -6 to 6
- green_occupied: bfloat16 [8, 3, 128, 128], P('ctr'), may hold values from -0.3125 to 0.3125
- green_virtual: bfloat16 [8, 3, 128, 128], P('ctr'), may hold values from -0.3125 to 0.3125
- block_sizes: int32 [8], replicated, may hold values from 64 to 128
- screening: int32 [8, 3], replicated, may hold values 0 or 1
Outputs:
- response: float32 [1024, 1024], P(('blk', 'ctr'))
The draws below stay inside these ranges and needn't reach their ends.
All inputs are finite; a program needn't handle non-finite values.
Results may differ from the reference program's by a relative error of at most 0.0041.
Values may be sent and summed in bfloat16 or wider, within the bound.
A program may use at most 128 MiB of HBM per device.

```python
import math
import jax
import jax.numpy as jnp
from jax import lax

BS = 128
NK = 3
NRI = 1024
NA = 8


def set_ends(result, key, least, largest):
    shape = result.shape
    spot = [jax.random.randint(jax.random.fold_in(key, axis), (), 0, shape[axis]) for axis in range(len(shape))]
    result = result.at[tuple(spot)].set(least)
    longest = shape.index(max(shape))
    spot[longest] = (spot[longest] + 1) % shape[longest]
    return result.at[tuple(spot)].set(largest)


def steps_of(key, dims, shards, smallest, largest):
    level = 1.0
    for axis_at, parts in shards:
        steps = jax.random.uniform(jax.random.fold_in(jax.random.fold_in(key, 6), axis_at), (parts,), jnp.float32, smallest / len(shards), largest / len(shards))
        level = level * jnp.repeat(jnp.exp(steps), dims[axis_at] // parts).reshape((-1,) + (1,) * (len(dims) - 1 - axis_at))
    return level


def scatter_about(rng, extent, deviation, limit, cuts=(), kind=jnp.bfloat16):
    result = jax.random.normal(rng, extent, jnp.float32) * deviation
    if len(cuts) > 0:
        result = steps_of(rng, extent, cuts, -0.22, 0.18) * result
    return jnp.clip(result, min=-limit, max=limit).astype(kind)


def setup_inputs(seed: int = 0) -> dict:
    key_of = jax.random.split(jax.random.key(seed), 6)
    return {
        "three_centre": scatter_about(key_of[0], (NA, BS, NK, NRI, BS), 1.0, 6.0, ((0, 8), (3, 16))),
        "green_occupied": scatter_about(key_of[1], (NA, NK, BS, BS), (NK * BS) ** -0.5, 0.3125, ((0, 8),)),
        "green_virtual": scatter_about(key_of[2], (NA, NK, BS, BS), (NK * BS) ** -0.5, 0.3125, ((0, 8),)),
        "block_sizes": set_ends(jax.random.randint(key_of[3], (NA,), BS // 2, BS + 1), jax.random.fold_in(key_of[3], 1), BS // 2, BS).astype(jnp.int32),
        "screening": set_ends((jax.random.randint(key_of[4], (NA, NK), 0, 4) < 3).astype(jnp.int32), jax.random.fold_in(key_of[4], 1), 0, 1),
    }


def masked_tensor(three_centre, block_sizes, screening):
    slots = jnp.arange(BS, dtype=jnp.int32)
    half = NK // 2
    row_valid = slots[None, :] < block_sizes[:, None]
    col_sizes = jnp.stack([jnp.roll(block_sizes, half - offset) for offset in range(NK)], axis=1)
    col_valid = slots[None, None, :] < col_sizes[:, :, None]
    kept = (screening == 1) | (jnp.arange(NK, dtype=jnp.int32) == half)[None, :]
    keep = row_valid[:, :, None, None, None] & kept[:, None, :, None, None] & col_valid[:, None, :, None, :]
    return jnp.where(keep, three_centre, jnp.zeros_like(three_centre))

def reference(three_centre, green_occupied, green_virtual, block_sizes, screening):
    masked = masked_tensor(three_centre, block_sizes, screening)
    half = NK // 2
    scale = -2.0 / (BS * math.sqrt(NA * NK))

    def one_atom(carry, atom):
        total = jnp.zeros((BS, 2 * NK - 1, NRI, BS), jnp.float32)
        for offset in range(NK):
            source = (atom + offset - half) % NA
            rows = masked[source].reshape(BS, NK * NRI * BS)
            term = jnp.dot(green_occupied[atom, offset], rows, preferred_element_type=jnp.float32)
            total = total.at[:, offset:offset + NK].add(term.reshape(BS, NK, NRI, BS))
        half_occ = total.astype(jnp.bfloat16)
        pieces = []
        for column in range(NK):
            target = (atom + column - half) % NA
            summed = jnp.zeros((BS * NRI, BS), jnp.float32)
            for inner in range(NK):
                left = half_occ[:, column + inner].reshape(BS * NRI, BS)
                summed = summed + jnp.dot(left, green_virtual[target, inner], preferred_element_type=jnp.float32)
            pieces.append(summed.reshape(BS, NRI, BS))
        both_half = jnp.stack(pieces, axis=1).astype(jnp.bfloat16)
        carry = carry + jnp.einsum('mopn,moqn->pq', masked[atom].astype(jnp.float32), both_half.astype(jnp.float32))
        return (carry, None)
    response, _ = lax.scan(one_atom, jnp.zeros((NRI, NRI), jnp.float32), jnp.arange(NA, dtype=jnp.int32))
    return response * scale
```

```python
import functools
import math

import jax
import jax.numpy as jnp
from jax import lax
from jax.experimental import pallas as pl
from jax.experimental.pallas import tpu as pltpu
from jax.sharding import PartitionSpec as P

MESH = pl.DeviceIdType.MESH
SIDE = 4
ROWS = 16

PLANE = (
    (0, 1), (0, 3), (1, 0), (3, 0),
    (1, 1), (3, 3), (1, 3), (3, 1),
    (0, 2), (2, 0), (2, 2),
    (1, 2), (3, 2), (2, 1), (2, 3),
)


def mm(a, b):
    return jnp.dot(a, b, preferred_element_type=jnp.float32)


def mm_nt(a, b):
    return lax.dot_general(a, b, (((1,), (1,)), ((), ())), preferred_element_type=jnp.float32)


def kernel(
    tc, go, gv, sizes, screen, out,
    own, halo, mrecv, bsend, brecv, gvn, gmat, gomat, vs, bsc, xsend, xrecv, ysend, yrecv,
    own_sem, slot_sem, gv_sems, halo_sems, m_sems, b_send_sem, b_recv_sem, b_own_sem,
    x_send_sem, x_recv_sem, y_send_sem, y_recv_sem,
):
    width, band, share, _ = tc.shape
    parts = share // ROWS
    nblk = mrecv.shape[0]
    nctr = lax.axis_size("ctr")
    rows = width // nblk
    blk, ctr = lax.axis_index("blk"), lax.axis_index("ctr")
    y, z = blk // SIDE, lax.rem(blk, SIDE)

    def peer(dy, dz):
        return lax.rem(y + dy, SIDE) * SIDE + lax.rem(z + dz, SIDE)

    def atom(shift):
        return lax.rem(ctr + shift + nctr, nctr)

    def send(src, dst, send_sem, recv_sem, b, c):
        pltpu.make_async_remote_copy(
            src_ref=src, dst_ref=dst, send_sem=send_sem, recv_sem=recv_sem,
            device_id=(b, c), device_id_type=MESH,
        ).start()

    def wait(ref, sem):
        pltpu.make_async_copy(ref, ref, sem).wait()

    def own_copy(part):
        slot = lax.rem(part, 2)
        return pltpu.make_async_copy(
            tc.at[:, :, pl.ds(part * ROWS, ROWS), :], own.at[slot], own_sem.at[slot]
        )

    own_copy(0).start()
    slot_copy = pltpu.make_async_copy(tc.at[pl.ds(blk * rows, rows)], mrecv.at[blk], slot_sem)
    slot_copy.start()

    barrier = pltpu.get_barrier_semaphore()
    for dy, dz in PLANE:
        pl.semaphore_signal(barrier, inc=1, device_id=(peer(dy, dz), ctr), device_id_type=MESH)
    for d in range(1, nctr):
        pl.semaphore_signal(barrier, inc=1, device_id=(blk, atom(d)), device_id_type=MESH)
    pl.semaphore_wait(barrier, len(PLANE) + nctr - 1)

    for slot, shift in ((0, 1), (1, -1)):
        send(gv, gvn.at[slot], gv_sems.at[0, slot], gv_sems.at[1, slot], blk, atom(shift))

    def first_sends(part, carry):
        piece = pl.ds(part * ROWS, ROWS)
        for slot, shift in ((0, 1), (1, -1)):
            send(
                tc.at[:, :, piece, :], halo.at[slot, part],
                halo_sems.at[0, slot, part], halo_sems.at[1, slot, part], blk, atom(shift),
            )
        for dy, dz in PLANE:
            b = peer(dy, dz)
            send(
                tc.at[pl.ds(b * rows, rows), :, piece, :], mrecv.at[blk, :, :, piece, :],
                m_sems.at[0], m_sems.at[1], b, ctr,
            )
        return carry

    lax.fori_loop(0, parts, first_sends, 0)

    r = lax.broadcasted_iota(jnp.int32, (width, width), 0)
    s = lax.broadcasted_iota(jnp.int32, (width, width), 1)
    for j in range(band):
        keep = (r < sizes[atom(0)]) & (s < sizes[atom(j - 1)])
        gomat[:, j * width : (j + 1) * width] = jnp.where(keep, go[j], jnp.zeros_like(go[j]))
    for slot in range(2):
        wait(gvn.at[slot], gv_sems.at[1, slot])
    for o in range(band):
        cols = s < sizes[atom(o - 1)]
        for j in range(band):
            for k in range(band):
                inner = j + k - o
                here = (j, pl.ds(k * width, width), pl.ds(o * width, width))
                if not 0 <= inner < band:
                    gmat[here] = jnp.zeros((width, width), gmat.dtype)
                    continue
                block = gv[inner] if o == 1 else gvn[o // 2, inner]
                keep = cols & (r < sizes[atom(j + k - 2)])
                if k != 1:
                    keep = keep & (screen[atom(j - 1), k] == 1)
                if o != 1:
                    keep = keep & (screen[atom(0), o] == 1)
                gmat[here] = jnp.where(keep, block, jnp.zeros_like(block))

    def transform(part, carry):
        slot = lax.rem(part, 2)
        own_copy(part).wait()

        @pl.when(part + 1 < parts)
        def _():
            own_copy(part + 1).start()

        step = 16
        for j in (1, 0, 2):
            if j != 1:
                wait(halo.at[j // 2, part], halo_sems.at[1, j // 2, part])

            def columns(t, carry):
                at = pl.ds(t * step, step)
                x = own[slot, at] if j == 1 else halo[j // 2, part, at]
                x = jnp.concatenate(
                    [x[:, k].reshape(step * ROWS, width) for k in range(band)], axis=1
                )
                v = mm(x, gmat[j])
                for o in range(band):
                    vs[j, o, pl.ds(t * step * ROWS, step * ROWS), :] = v[:, o * width : (o + 1) * width]
                return carry

            lax.fori_loop(0, width // step, columns, 0)

        def occupied(p, carry):
            at = pl.ds(p, width, stride=ROWS)
            right = jnp.concatenate(
                [
                    jnp.concatenate(
                        [vs[j, o, at, :].astype(jnp.bfloat16) for o in range(band)], axis=1
                    )
                    for j in range(band)
                ],
                axis=0,
            )
            b = mm(gomat[...], right)
            for o in range(band):
                bsc[o, at, :] = b[:, o * width : (o + 1) * width]
            return carry

        lax.fori_loop(0, ROWS, occupied, 0)

        def rounded(i, carry):
            for o in range(band):
                b = bsc[o, pl.ds(i * rows * ROWS, rows * ROWS), :].astype(jnp.bfloat16)
                bsend[part, i, :, o] = b.reshape(rows, ROWS, width)
            return carry

        lax.fori_loop(0, nblk, rounded, 0)
        for dy, dz in PLANE:
            b = peer(dy, dz)
            send(bsend.at[part, b], brecv.at[part, blk], b_send_sem, b_recv_sem.at[part], b, ctr)
        pltpu.make_async_copy(bsend.at[part, blk], brecv.at[part, blk], b_own_sem.at[part]).start()
        return carry

    lax.fori_loop(0, parts, transform, 0)

    slot_copy.wait()
    wait(mrecv.at[pl.ds(0, nblk - 1)], m_sems.at[1])

    def product(part, carry):
        pltpu.make_async_copy(bsend.at[part, blk], brecv.at[part, blk], b_own_sem.at[part]).wait()
        wait(brecv.at[part, pl.ds(0, nblk - 1)], b_recv_sem.at[part])
        group = 4

        def tile(t, carry):
            at = pl.ds(t * group, group)
            acc = None
            for m0 in range(0, rows, 2):
                pairs = [(m, o) for m in (m0, m0 + 1) for o in range(band)]
                left = jnp.concatenate(
                    [mrecv[at, m, o].reshape(group * share, width) for m, o in pairs], axis=1
                )
                right = jnp.concatenate(
                    [brecv[part, :, m, o].reshape(nblk * ROWS, width) for m, o in pairs], axis=1
                )
                term = mm_nt(left, right)
                acc = term if acc is None else acc + term
            acc = acc.reshape(group, nctr, 8, nblk * ROWS)
            for c in range(nctr):
                xsend[part, c, pl.ds(t * group * 8, group * 8), :] = acc[:, c].reshape(
                    group * 8, nblk * ROWS
                )
            return carry

        lax.fori_loop(0, nblk // group, tile, 0)
        for d in range(1, nctr):
            c = atom(d)
            send(xsend.at[part, c], xrecv.at[part, d - 1], x_send_sem, x_recv_sem.at[part], blk, c)

        @pl.when(part > 0)
        def _():
            reduce(part - 1)

        return carry

    def reduce(part):
        wait(xrecv.at[part], x_recv_sem.at[part])
        total = xsend[part, ctr]
        for d in range(nctr - 1):
            total = total + xrecv[part, d]
        ysend[part] = total
        for n, (dy, dz) in enumerate(PLANE):
            b = peer(dy, dz)
            send(ysend.at[part, pl.ds(b * 8, 8), :], yrecv.at[part, n], y_send_sem, y_recv_sem, b, ctr)

    lax.fori_loop(0, parts, product, 0)
    reduce(parts - 1)

    scale = -2.0 / (width * math.sqrt(nctr * band))
    wait(yrecv, y_recv_sem)
    for part in range(parts):
        total = ysend[part, pl.ds(pl.multiple_of(blk * 8, 8), 8), :]
        for n in range(nblk - 1):
            total = total + yrecv[part, n]
        out[part] = total * scale

    for slot in range(2):
        wait(gvn.at[slot], gv_sems.at[0, slot])
        for part in range(parts):
            wait(halo.at[slot, part], halo_sems.at[0, slot, part])
    wait(mrecv.at[pl.ds(0, nblk - 1)], m_sems.at[0])
    wait(brecv.at[:, pl.ds(0, nblk - 1)], b_send_sem)
    wait(xrecv, x_send_sem)
    wait(yrecv, y_send_sem)


def per_device(three_centre, green_occupied, green_virtual, block_sizes, screening):
    _, width, band, share, _ = three_centre.shape
    nblk, nctr = lax.axis_size("blk"), lax.axis_size("ctr")
    parts, rows, cols = share // ROWS, width // nblk, nblk * ROWS
    bf16, f32 = jnp.bfloat16, jnp.float32
    vmem, dma = pltpu.VMEM, pltpu.SemaphoreType.DMA
    got = pl.pallas_call(
        kernel,
        out_shape=jax.ShapeDtypeStruct((parts, 8, cols), f32),
        in_specs=[
            pl.BlockSpec(memory_space=pl.ANY),
            pl.BlockSpec(memory_space=pltpu.VMEM),
            pl.BlockSpec(memory_space=pltpu.VMEM),
            pl.BlockSpec(memory_space=pltpu.SMEM),
            pl.BlockSpec(memory_space=pltpu.SMEM),
        ],
        out_specs=pl.BlockSpec(memory_space=pltpu.VMEM),
        scratch_shapes=[
            vmem((2, width, band, ROWS, width), bf16),
            vmem((2, parts, width, band, ROWS, width), bf16),
            vmem((nblk, rows, band, share, width), bf16),
            vmem((parts, nblk, rows, band, ROWS, width), bf16),
            vmem((parts, nblk, rows, band, ROWS, width), bf16),
            vmem((2, band, width, width), bf16),
            vmem((band, band * width, band * width), bf16),
            vmem((width, band * width), bf16),
            vmem((band, band, width * ROWS, width), f32),
            vmem((band, width * ROWS, width), f32),
            vmem((parts, nctr, nblk * 8, cols), f32),
            vmem((parts, nctr - 1, nblk * 8, cols), f32),
            vmem((parts, nblk * 8, cols), f32),
            vmem((parts, nblk - 1, 8, cols), f32),
            dma((2,)),
            dma,
            dma((2, 2)),
            dma((2, 2, parts)),
            dma((2,)),
            dma,
            dma((parts,)),
            dma((parts,)),
            dma,
            dma((parts,)),
            dma,
            dma,
        ],
        compiler_params=pltpu.CompilerParams(
            collective_id=0, has_side_effects=True, vmem_limit_bytes=62 << 20
        ),
        name="response",
    )(three_centre[0], green_occupied[0], green_virtual[0], block_sizes, screening)
    got = got.reshape(parts, 8, nblk, ROWS)
    return got.transpose(1, 2, 0, 3).reshape(8, nblk * share)


def solution(mesh):
    return jax.shard_map(
        per_device,
        mesh=mesh,
        in_specs=(
            P("ctr", None, None, "blk", None),
            P("ctr", None, None, None),
            P("ctr", None, None, None),
            P(),
            P(),
        ),
        out_specs=P(("blk", "ctr"), None),
        check_vma=False,
    )
```

```python
import functools
import math

import jax
import jax.numpy as jnp
from jax import lax
from jax.experimental import pallas as pl
from jax.experimental.pallas import tpu as pltpu
from jax.sharding import PartitionSpec as P

MESH = pl.DeviceIdType.MESH
SIDE = 4
ROWS = 16
TILES = 4
LANES = 128

PLANE = (
    (2, 2), (1, 2), (3, 2), (2, 1), (2, 3),
    (0, 2), (2, 0), (1, 1), (3, 3), (1, 3), (3, 1),
    (0, 1), (0, 3), (1, 0), (3, 0),
)


def mm(a, b):
    return jnp.dot(a, b, preferred_element_type=jnp.float32)


def mm_nt(a, b):
    return lax.dot_general(a, b, (((1,), (1,)), ((), ())), preferred_element_type=jnp.float32)


def kernel(
    tc, go_hbm, gv_hbm, sizes, screen, out,
    own, halo, mrecv, bsend, brecv, go, gvn, gmat, gomat, vs, bsc,
    xsend, xrecv, xsend_last, xrecv_last, ysend, yrecv,
    in_sems, own_sem, slot_sem, gv_sems, halo_sems, m_sems, b_send_sem, b_recv_sem, b_own_sem,
    x_send_sems, x_recv_sem, y_send_sem, y_recv_sem,
):
    width, band, share, _ = tc.shape
    parts = share // ROWS
    nblk = mrecv.shape[0]
    nctr = lax.axis_size("ctr")
    rows = width // nblk
    blk, ctr = lax.axis_index("blk"), lax.axis_index("ctr")
    y, z = blk // SIDE, lax.rem(blk, SIDE)

    def peer(dy, dz):
        return lax.rem(y + dy, SIDE) * SIDE + lax.rem(z + dz, SIDE)

    def atom(shift):
        return lax.rem(ctr + shift + nctr, nctr)

    def send(src, dst, send_sem, recv_sem, b, c):
        pltpu.make_async_remote_copy(
            src_ref=src, dst_ref=dst, send_sem=send_sem, recv_sem=recv_sem,
            device_id=(b, c), device_id_type=MESH,
        ).start()

    def wait(ref, sem):
        pltpu.make_async_copy(ref, ref, sem).wait()

    def own_copy(part):
        slot = lax.rem(part, 2)
        return pltpu.make_async_copy(
            tc.at[:, :, pl.ds(part * ROWS, ROWS), :], own.at[slot], own_sem.at[slot]
        )

    inputs = [
        pltpu.make_async_copy(src, dst, in_sems.at[n])
        for n, (src, dst) in enumerate(
            ((go_hbm, go), (gv_hbm, gvn.at[1]))
        )
    ]
    for copy in inputs:
        copy.start()
    own_copy(0).start()
    slot_copy = pltpu.make_async_copy(tc.at[pl.ds(blk * rows, rows)], mrecv.at[blk], slot_sem)
    slot_copy.start()

    barrier = pltpu.get_barrier_semaphore()
    for dy, dz in PLANE:
        pl.semaphore_signal(barrier, inc=1, device_id=(peer(dy, dz), ctr), device_id_type=MESH)
    for d in range(1, nctr):
        pl.semaphore_signal(barrier, inc=1, device_id=(blk, atom(d)), device_id_type=MESH)
    pl.semaphore_wait(barrier, len(PLANE) + nctr - 1)

    for slot, shift in ((0, 1), (1, -1)):
        send(
            gv_hbm, gvn.at[2 * slot], gv_sems.at[0, slot], gv_sems.at[1, slot], blk, atom(shift)
        )

    def first_sends(part, carry):
        piece = pl.ds(part * ROWS, ROWS)
        for slot, shift in ((0, 1), (1, -1)):
            send(
                tc.at[:, :, piece, :], halo.at[slot, part],
                halo_sems.at[0, slot, part], halo_sems.at[1, slot, part], blk, atom(shift),
            )
        for cut in range(2):
            some = rows // 2
            for dy, dz in PLANE:
                b = peer(dy, dz)
                send(
                    tc.at[pl.ds(b * rows + cut * some, some), :, piece, :],
                    mrecv.at[blk, pl.ds(cut * some, some), :, piece, :],
                    m_sems.at[0], m_sems.at[1], b, ctr,
                )
        return carry

    lax.fori_loop(0, parts, first_sends, 0)

    r = lax.broadcasted_iota(jnp.int32, (width, width), 0)
    s = lax.broadcasted_iota(jnp.int32, (width, width), 1)
    for copy in inputs:
        copy.wait()
    for j in range(band):
        keep = (r < sizes[atom(0)]) & (s < sizes[atom(j - 1)])
        gomat[:, j * width : (j + 1) * width] = jnp.where(keep, go[j], jnp.zeros_like(go[j]))
    for slot in range(2):
        wait(gvn.at[2 * slot], gv_sems.at[1, slot])

    for o in range(band):
        cols = s < sizes[atom(o - 1)]
        for j in range(band):
            for k in range(band):
                inner = j + k - o
                here = (j, pl.ds(k * width, width), pl.ds(o * width, width))
                if not 0 <= inner < band:
                    gmat[here] = jnp.zeros((width, width), gmat.dtype)
                    continue
                block = gvn[o, inner]
                keep = cols & (r < sizes[atom(j + k - 2)])
                if k != 1:
                    keep = keep & (screen[k, atom(j - 1)] == 1)
                if o != 1:
                    keep = keep & (screen[o, atom(0)] == 1)
                gmat[here] = jnp.where(keep, block, jnp.zeros_like(block))

    def second_sends(part):
        for cut in range(2):
            some = pl.ds(cut * (rows // 2), rows // 2)
            for dy, dz in PLANE:
                b = peer(dy, dz)
                send(
                    bsend.at[part, b, some], brecv.at[part, blk, some],
                    b_send_sem, b_recv_sem.at[part], b, ctr,
                )
        pltpu.make_async_copy(bsend.at[part, blk], brecv.at[part, blk], b_own_sem.at[part]).start()

    def transform(part, carry):
        slot = lax.rem(part, 2)
        own_copy(part).wait()

        @pl.when(part + 1 < parts)
        def _():
            own_copy(part + 1).start()

        step = 16
        for j in (1, 0, 2):
            if j != 1:
                wait(halo.at[j // 2, part], halo_sems.at[1, j // 2, part])

            def columns(t, carry):
                at = pl.ds(t * step, step)
                x = own[slot, at] if j == 1 else halo[j // 2, part, at]
                x = jnp.concatenate(
                    [x[:, k].reshape(step * ROWS, width) for k in range(band)], axis=1
                )
                v = mm(x, gmat[j])
                for o in range(band):
                    vs[j, o, pl.ds(t * step * ROWS, step * ROWS), :] = v[:, o * width : (o + 1) * width]
                return carry

            lax.fori_loop(0, width // step, columns, 0)

        def occupied(p, carry):
            at = pl.ds(p, width, stride=ROWS)
            right = jnp.concatenate(
                [
                    jnp.concatenate(
                        [vs[j, o, at, :].astype(jnp.bfloat16) for o in range(band)], axis=1
                    )
                    for j in range(band)
                ],
                axis=0,
            )
            b = mm(gomat[...], right)
            for o in range(band):
                bsc[o, at, :] = b[:, o * width : (o + 1) * width]
            return carry

        lax.fori_loop(0, ROWS, occupied, 0)

        def rounded(i, carry):
            for o in range(band):
                b = bsc[o, pl.ds(i * rows * ROWS, rows * ROWS), :].astype(jnp.bfloat16)
                bsend[part, i, :, o] = b.reshape(rows, ROWS, width)
            return carry

        lax.fori_loop(0, nblk, rounded, 0)

        @pl.when(part > 0)
        def _():
            second_sends(part - 1)

        return carry

    lax.fori_loop(0, parts, transform, 0)

    slot_copy.wait()
    wait(mrecv.at[pl.ds(0, nblk - 1)], m_sems.at[1])

    group = nblk // TILES
    cols = nblk * ROWS
    last = parts - 1

    def first(t):
        return lax.rem(y + t, TILES) * group

    def product(part, sent, got, send_sem):
        pltpu.make_async_copy(bsend.at[part, blk], brecv.at[part, blk], b_own_sem.at[part]).wait()
        wait(brecv.at[part, pl.ds(0, nblk - 1)], b_recv_sem.at[part])

        def tile(t, carry):
            at = pl.ds(first(t), group)
            here = pl.ds(pl.multiple_of(t * group * 8, group * 8), group * 8)
            acc = None
            for m0 in range(0, rows, 2):
                pairs = [(m, o) for m in (m0, m0 + 1) for o in range(band)]
                left = jnp.concatenate(
                    [mrecv[at, m, o].reshape(group * share, width) for m, o in pairs], axis=1
                )
                right = jnp.concatenate(
                    [brecv[part, :, m, o].reshape(cols, width) for m, o in pairs], axis=1
                )
                term = mm_nt(left, right)
                acc = term if acc is None else acc + term
            acc = acc.reshape(group, nctr, 8, cols)
            for c in range(nctr):
                sent[c, here, :] = acc[:, c].reshape(group * 8, cols).astype(sent.dtype)
            for d in range(1, nctr):
                c = atom(d)
                send(
                    sent.at[c, here, :], got.at[d - 1, here, :],
                    send_sem, x_recv_sem.at[part, t], blk, c,
                )
            return carry

        lax.fori_loop(0, TILES, tile, 0)

    def reduce(part, sent, got):
        def tile(t, carry):
            here = pl.ds(pl.multiple_of(t * group * 8, group * 8), group * 8)
            wait(got.at[:, here, :], x_recv_sem.at[part, t])
            total = sent[ctr, here, :].astype(jnp.float32)
            for d in range(nctr - 1):
                total = total + got[d, here, :].astype(jnp.float32)
            ysend[part, here, :] = total
            for i in range(group):
                b = first(t) + i
                row = pl.ds(pl.multiple_of((t * group + i) * 8, 8), 8)

                @pl.when(b == blk)
                def _():
                    yrecv[part, blk] = ysend[part, row, :]

                @pl.when(b != blk)
                def _():
                    send(ysend.at[part, row, :], yrecv.at[part, blk], y_send_sem, y_recv_sem, b, ctr)

            return carry

        lax.fori_loop(0, TILES, tile, 0)

    def middle(part, carry):
        product(part, xsend.at[part], xrecv.at[part], x_send_sems.at[0])

        @pl.when(part == 1)
        def _():
            second_sends(last)

        @pl.when(part > 0)
        def _():
            reduce(part - 1, xsend.at[part - 1], xrecv.at[part - 1])

        return carry

    lax.fori_loop(0, last, middle, 0)
    product(last, xsend_last, xrecv_last, x_send_sems.at[1])
    reduce(last - 1, xsend.at[last - 1], xrecv.at[last - 1])
    reduce(last, xsend_last, xrecv_last)

    scale = -2.0 / (width * math.sqrt(nctr * band))
    wait(yrecv.at[:, pl.ds(0, nblk - 1)], y_recv_sem)
    lane = lax.broadcasted_iota(jnp.int32, (8, LANES), 1)
    held = [jnp.zeros((8, LANES), jnp.float32) for _ in range(nblk * share // LANES)]
    for part in range(parts):
        total = yrecv[part, 0]
        for n in range(1, nblk):
            total = total + yrecv[part, n]
        total = total * scale
        for n in range(nblk):
            at, to = n * ROWS, n * share + part * ROWS
            piece = total[:, at // LANES * LANES : (at // LANES + 1) * LANES]
            shift = (to - at) % LANES
            if shift:
                piece = pltpu.roll(piece, shift, 1)
            here = (lane >= to % LANES) & (lane < to % LANES + ROWS)
            held[to // LANES] = jnp.where(here, piece, held[to // LANES])
    for n, piece in enumerate(held):
        out[:, n * LANES : (n + 1) * LANES] = piece

    for slot in range(2):
        wait(gvn.at[2 * slot], gv_sems.at[0, slot])
        for part in range(parts):
            wait(halo.at[slot, part], halo_sems.at[0, slot, part])
    wait(mrecv.at[pl.ds(0, nblk - 1)], m_sems.at[0])
    wait(brecv.at[:, pl.ds(0, nblk - 1)], b_send_sem)
    wait(xrecv, x_send_sems.at[0])
    wait(xrecv_last, x_send_sems.at[1])
    wait(yrecv.at[:, pl.ds(0, nblk - 1)], y_send_sem)


def per_device(three_centre, green_occupied, green_virtual, block_sizes, screening):
    _, width, band, share, _ = three_centre.shape
    nblk, nctr = lax.axis_size("blk"), lax.axis_size("ctr")
    parts, rows, cols = share // ROWS, width // nblk, nblk * ROWS
    bf16, f32 = jnp.bfloat16, jnp.float32
    vmem, dma = pltpu.VMEM, pltpu.SemaphoreType.DMA
    return pl.pallas_call(
        kernel,
        out_shape=jax.ShapeDtypeStruct((8, nblk * share), f32),
        in_specs=[
            pl.BlockSpec(memory_space=pl.ANY),
            pl.BlockSpec(memory_space=pl.ANY),
            pl.BlockSpec(memory_space=pl.ANY),
            pl.BlockSpec(memory_space=pltpu.SMEM),
            pl.BlockSpec(memory_space=pltpu.SMEM),
        ],
        out_specs=pl.BlockSpec(memory_space=pltpu.VMEM),
        scratch_shapes=[
            vmem((2, width, band, ROWS, width), bf16),
            vmem((2, parts, width, band, ROWS, width), bf16),
            vmem((nblk, rows, band, share, width), bf16),
            vmem((parts, nblk, rows, band, ROWS, width), bf16),
            vmem((parts, nblk, rows, band, ROWS, width), bf16),
            vmem((band, width, width), bf16),
            vmem((3, band, width, width), bf16),
            vmem((band, band * width, band * width), bf16),
            vmem((width, band * width), bf16),
            vmem((band, band, width * ROWS, width), f32),
            vmem((band, width * ROWS, width), f32),
            vmem((parts - 1, nctr, nblk * 8, cols), f32),
            vmem((parts - 1, nctr - 1, nblk * 8, cols), f32),
            vmem((nctr, nblk * 8, cols), bf16),
            vmem((nctr - 1, nblk * 8, cols), bf16),
            vmem((parts, nblk * 8, cols), f32),
            vmem((parts, nblk, 8, cols), f32),
            dma((2,)),
            dma((2,)),
            dma,
            dma((2, 2)),
            dma((2, 2, parts)),
            dma((2,)),
            dma,
            dma((parts,)),
            dma((parts,)),
            dma((2,)),
            dma((parts, TILES)),
            dma,
            dma,
        ],
        compiler_params=pltpu.CompilerParams(
            collective_id=0, has_side_effects=True, vmem_limit_bytes=62 << 20
        ),
        name="response",
    )(three_centre[0], green_occupied[0], green_virtual[0], block_sizes, screening.T)


def solution(mesh):
    return jax.shard_map(
        per_device,
        mesh=mesh,
        in_specs=(
            P("ctr", None, None, "blk", None),
            P("ctr", None, None, None),
            P("ctr", None, None, None),
            P(),
            P(),
        ),
        out_specs=P(("blk", "ctr"), None),
        check_vma=False,
    )
```

```python
import functools
import math

import jax
import jax.numpy as jnp
from jax import lax
from jax.experimental import pallas as pl
from jax.experimental.pallas import tpu as pltpu
from jax.sharding import PartitionSpec as P

MESH = pl.DeviceIdType.MESH
SIDE = 4
ROWS = 16
TILES = 4
LANES = 128
AT_ONCE = 4

PLANE = (
    (2, 2), (1, 2), (3, 2), (2, 1), (2, 3),
    (0, 2), (2, 0), (1, 1), (3, 3), (1, 3), (3, 1),
    (0, 1), (0, 3), (1, 0), (3, 0),
)


def mm(a, b):
    return jnp.dot(a, b, preferred_element_type=jnp.float32)


def mm_nt(a, b):
    return lax.dot_general(a, b, (((1,), (1,)), ((), ())), preferred_element_type=jnp.float32)


def kernel(
    tc, go_hbm, gv_hbm, sizes, screen, out,
    own, halo, mrecv, bsend, brecv, go, gvn, gmat, gomat, ms, bsc,
    xsend, xrecv, xsend_last, xrecv_last, ysend, yrecv,
    in_sems, own_sem, slot_sem, gv_sems, halo_sems, m_sems, b_send_sem, b_recv_sem, b_own_sem,
    x_send_sems, x_recv_sem, y_send_sem, y_recv_sem,
):
    width, band, share, _ = tc.shape
    parts = share // ROWS
    nblk = mrecv.shape[0]
    nctr = lax.axis_size("ctr")
    rows = width // nblk
    blk, ctr = lax.axis_index("blk"), lax.axis_index("ctr")
    y, z = blk // SIDE, lax.rem(blk, SIDE)

    def peer(dy, dz):
        return lax.rem(y + dy, SIDE) * SIDE + lax.rem(z + dz, SIDE)

    def atom(shift):
        return lax.rem(ctr + shift + nctr, nctr)

    def send(src, dst, send_sem, recv_sem, b, c):
        pltpu.make_async_remote_copy(
            src_ref=src, dst_ref=dst, send_sem=send_sem, recv_sem=recv_sem,
            device_id=(b, c), device_id_type=MESH,
        ).start()

    def wait(ref, sem):
        pltpu.make_async_copy(ref, ref, sem).wait()

    def own_copy(part):
        slot = lax.rem(part, 2)
        return pltpu.make_async_copy(
            tc.at[:, :, pl.ds(part * ROWS, ROWS), :], own.at[slot], own_sem.at[slot]
        )

    inputs = [
        pltpu.make_async_copy(src, dst, in_sems.at[n])
        for n, (src, dst) in enumerate(
            ((go_hbm, go), (gv_hbm, gvn.at[1]))
        )
    ]
    for copy in inputs:
        copy.start()
    own_copy(0).start()
    slot_copy = pltpu.make_async_copy(tc.at[pl.ds(blk * rows, rows)], mrecv.at[blk], slot_sem)
    slot_copy.start()

    barrier = pltpu.get_barrier_semaphore()
    for dy, dz in PLANE:
        pl.semaphore_signal(barrier, inc=1, device_id=(peer(dy, dz), ctr), device_id_type=MESH)
    for d in range(1, nctr):
        pl.semaphore_signal(barrier, inc=1, device_id=(blk, atom(d)), device_id_type=MESH)
    pl.semaphore_wait(barrier, len(PLANE) + nctr - 1)

    for slot, shift in ((0, 1), (1, -1)):
        send(
            gv_hbm, gvn.at[2 * slot], gv_sems.at[0, slot], gv_sems.at[1, slot], blk, atom(shift)
        )

    def first_sends(part, carry):
        piece = pl.ds(part * ROWS, ROWS)
        for slot, shift in ((0, 1), (1, -1)):
            send(
                tc.at[:, :, piece, :], halo.at[slot, part],
                halo_sems.at[0, slot, part], halo_sems.at[1, slot, part], blk, atom(shift),
            )
        for cut in range(2):
            some = rows // 2
            for dy, dz in PLANE:
                b = peer(dy, dz)
                send(
                    tc.at[pl.ds(b * rows + cut * some, some), :, piece, :],
                    mrecv.at[blk, pl.ds(cut * some, some), :, piece, :],
                    m_sems.at[0], m_sems.at[1], b, ctr,
                )
        return carry

    lax.fori_loop(0, parts, first_sends, 0)

    wide = 2 * band - 1
    terms = [(e, j) for e in range(wide) for j in range(band) if 0 <= e - j < band]
    r = lax.broadcasted_iota(jnp.int32, (width, width), 0)
    s = lax.broadcasted_iota(jnp.int32, (width, width), 1)
    for copy in inputs:
        copy.wait()
    for n, (e, j) in enumerate(terms):
        k = e - j
        keep = (r < sizes[atom(0)]) & (s < sizes[atom(j - 1)])
        if k != 1:
            keep = keep & (screen[k, atom(j - 1)] == 1)
        gomat[:, n * width : (n + 1) * width] = jnp.where(keep, go[j], jnp.zeros_like(go[j]))
    for slot in range(2):
        wait(gvn.at[2 * slot], gv_sems.at[1, slot])

    for e in range(wide):
        for o in range(band):
            here = (pl.ds(e * width, width), pl.ds(o * width, width))
            if not 0 <= e - o < band:
                gmat[here] = jnp.zeros((width, width), gmat.dtype)
                continue
            keep = (r < sizes[atom(e - 2)]) & (s < sizes[atom(o - 1)])
            if o != 1:
                keep = keep & (screen[o, atom(0)] == 1)
            gmat[here] = jnp.where(keep, gvn[o, e - o], jnp.zeros((width, width), gmat.dtype))

    def second_sends(part):
        for cut in range(2):
            some = pl.ds(cut * (rows // 2), rows // 2)
            for dy, dz in PLANE:
                b = peer(dy, dz)
                send(
                    bsend.at[part, b, some], brecv.at[part, blk, some],
                    b_send_sem, b_recv_sem.at[part], b, ctr,
                )
        pltpu.make_async_copy(bsend.at[part, blk], brecv.at[part, blk], b_own_sem.at[part]).start()

    def transform(part, carry):
        slot = lax.rem(part, 2)
        own_copy(part).wait()

        @pl.when(part + 1 < parts)
        def _():
            own_copy(part + 1).start()

        step = 16
        for j in (1, 0, 2):
            if j != 1:
                wait(halo.at[j // 2, part], halo_sems.at[1, j // 2, part])

            def columns(t, carry):
                at = pl.ds(t * step, step)
                x = own[slot, at] if j == 1 else halo[j // 2, part, at]
                for k in range(band):
                    y = x[:, k].reshape(step * ROWS, width).astype(jnp.float32)
                    ms[j, k, pl.ds(t * step * ROWS, step * ROWS), :] = y
                return carry

            lax.fori_loop(0, width // step, columns, 0)

        def green(g, carry):
            places = [pl.ds(g * AT_ONCE + p, width, stride=ROWS) for p in range(AT_ONCE)]
            half = []
            for e in range(wide):
                js = [n for n, (of, _) in enumerate(terms) if of == e]
                right = jnp.concatenate(
                    [
                        jnp.concatenate(
                            [
                                ms[terms[n][1], e - terms[n][1], at, :].astype(jnp.bfloat16)
                                for at in places
                            ],
                            axis=1,
                        )
                        for n in js
                    ],
                    axis=0,
                )
                left = gomat[:, js[0] * width : (js[-1] + 1) * width]
                half.append(mm(left, right).astype(jnp.bfloat16))
            left = jnp.concatenate(
                [
                    jnp.concatenate([h[:, p * width : (p + 1) * width] for h in half], axis=1)
                    for p in range(AT_ONCE)
                ],
                axis=0,
            )
            b = mm(left, gmat[...])
            for p, at in enumerate(places):
                for o in range(band):
                    bsc[o, at, :] = b[p * width : (p + 1) * width, o * width : (o + 1) * width]
            return carry

        lax.fori_loop(0, ROWS // AT_ONCE, green, 0)

        def rounded(i, carry):
            for o in range(band):
                b = bsc[o, pl.ds(i * rows * ROWS, rows * ROWS), :].astype(jnp.bfloat16)
                bsend[part, i, :, o] = b.reshape(rows, ROWS, width)
            return carry

        lax.fori_loop(0, nblk, rounded, 0)

        @pl.when(part > 0)
        def _():
            second_sends(part - 1)

        return carry

    lax.fori_loop(0, parts, transform, 0)

    slot_copy.wait()
    wait(mrecv.at[pl.ds(0, nblk - 1)], m_sems.at[1])

    group = nblk // TILES
    cols = nblk * ROWS
    last = parts - 1

    def first(t):
        return lax.rem(y + t, TILES) * group

    def product(part, sent, got, send_sem):
        pltpu.make_async_copy(bsend.at[part, blk], brecv.at[part, blk], b_own_sem.at[part]).wait()
        wait(brecv.at[part, pl.ds(0, nblk - 1)], b_recv_sem.at[part])

        def tile(t, carry):
            at = pl.ds(first(t), group)
            here = pl.ds(pl.multiple_of(t * group * 8, group * 8), group * 8)
            acc = None
            for m0 in range(0, rows, 2):
                pairs = [(m, o) for m in (m0, m0 + 1) for o in range(band)]
                left = jnp.concatenate(
                    [mrecv[at, m, o].reshape(group * share, width) for m, o in pairs], axis=1
                )
                right = jnp.concatenate(
                    [brecv[part, :, m, o].reshape(cols, width) for m, o in pairs], axis=1
                )
                term = mm_nt(left, right)
                acc = term if acc is None else acc + term
            acc = acc.reshape(group, nctr, 8, cols)
            for c in range(nctr):
                sent[c, here, :] = acc[:, c].reshape(group * 8, cols).astype(sent.dtype)
            for d in range(1, nctr):
                c = atom(d)
                send(
                    sent.at[c, here, :], got.at[d - 1, here, :],
                    send_sem, x_recv_sem.at[part, t], blk, c,
                )
            return carry

        lax.fori_loop(0, TILES, tile, 0)

    def reduce(part, sent, got):
        def tile(t, carry):
            here = pl.ds(pl.multiple_of(t * group * 8, group * 8), group * 8)
            wait(got.at[:, here, :], x_recv_sem.at[part, t])
            total = sent[ctr, here, :].astype(jnp.float32)
            for d in range(nctr - 1):
                total = total + got[d, here, :].astype(jnp.float32)
            ysend[part, here, :] = total
            for i in range(group):
                b = first(t) + i
                row = pl.ds(pl.multiple_of((t * group + i) * 8, 8), 8)

                @pl.when(b == blk)
                def _():
                    yrecv[part, blk] = ysend[part, row, :]

                @pl.when(b != blk)
                def _():
                    send(ysend.at[part, row, :], yrecv.at[part, blk], y_send_sem, y_recv_sem, b, ctr)

            return carry

        lax.fori_loop(0, TILES, tile, 0)

    def middle(part, carry):
        product(part, xsend.at[part], xrecv.at[part], x_send_sems.at[0])

        @pl.when(part == 1)
        def _():
            second_sends(last)

        @pl.when(part > 0)
        def _():
            reduce(part - 1, xsend.at[part - 1], xrecv.at[part - 1])

        return carry

    lax.fori_loop(0, last, middle, 0)
    product(last, xsend_last, xrecv_last, x_send_sems.at[1])
    reduce(last - 1, xsend.at[last - 1], xrecv.at[last - 1])
    reduce(last, xsend_last, xrecv_last)

    scale = -2.0 / (width * math.sqrt(nctr * band))
    wait(yrecv.at[:, pl.ds(0, nblk - 1)], y_recv_sem)
    lane = lax.broadcasted_iota(jnp.int32, (8, LANES), 1)
    held = [jnp.zeros((8, LANES), jnp.float32) for _ in range(nblk * share // LANES)]
    for part in range(parts):
        total = yrecv[part, 0]
        for n in range(1, nblk):
            total = total + yrecv[part, n]
        total = total * scale
        for n in range(nblk):
            at, to = n * ROWS, n * share + part * ROWS
            piece = total[:, at // LANES * LANES : (at // LANES + 1) * LANES]
            shift = (to - at) % LANES
            if shift:
                piece = pltpu.roll(piece, shift, 1)
            here = (lane >= to % LANES) & (lane < to % LANES + ROWS)
            held[to // LANES] = jnp.where(here, piece, held[to // LANES])
    for n, piece in enumerate(held):
        out[:, n * LANES : (n + 1) * LANES] = piece

    for slot in range(2):
        wait(gvn.at[2 * slot], gv_sems.at[0, slot])
        for part in range(parts):
            wait(halo.at[slot, part], halo_sems.at[0, slot, part])
    wait(mrecv.at[pl.ds(0, nblk - 1)], m_sems.at[0])
    wait(brecv.at[:, pl.ds(0, nblk - 1)], b_send_sem)
    wait(xrecv, x_send_sems.at[0])
    wait(xrecv_last, x_send_sems.at[1])
    wait(yrecv.at[:, pl.ds(0, nblk - 1)], y_send_sem)


def per_device(three_centre, green_occupied, green_virtual, block_sizes, screening):
    _, width, band, share, _ = three_centre.shape
    nblk, nctr = lax.axis_size("blk"), lax.axis_size("ctr")
    parts, rows, cols = share // ROWS, width // nblk, nblk * ROWS
    bf16, f32 = jnp.bfloat16, jnp.float32
    vmem, dma = pltpu.VMEM, pltpu.SemaphoreType.DMA
    return pl.pallas_call(
        kernel,
        out_shape=jax.ShapeDtypeStruct((8, nblk * share), f32),
        in_specs=[
            pl.BlockSpec(memory_space=pl.ANY),
            pl.BlockSpec(memory_space=pl.ANY),
            pl.BlockSpec(memory_space=pl.ANY),
            pl.BlockSpec(memory_space=pltpu.SMEM),
            pl.BlockSpec(memory_space=pltpu.SMEM),
        ],
        out_specs=pl.BlockSpec(memory_space=pltpu.VMEM),
        scratch_shapes=[
            vmem((2, width, band, ROWS, width), bf16),
            vmem((2, parts, width, band, ROWS, width), bf16),
            vmem((nblk, rows, band, share, width), bf16),
            vmem((parts, nblk, rows, band, ROWS, width), bf16),
            vmem((parts, nblk, rows, band, ROWS, width), bf16),
            vmem((band, width, width), bf16),
            vmem((3, band, width, width), bf16),
            vmem(((2 * band - 1) * width, band * width), bf16),
            vmem((width, band * band * width), bf16),
            vmem((band, band, width * ROWS, width), f32),
            vmem((band, width * ROWS, width), f32),
            vmem((parts - 1, nctr, nblk * 8, cols), f32),
            vmem((parts - 1, nctr - 1, nblk * 8, cols), f32),
            vmem((nctr, nblk * 8, cols), bf16),
            vmem((nctr - 1, nblk * 8, cols), bf16),
            vmem((parts, nblk * 8, cols), f32),
            vmem((parts, nblk, 8, cols), f32),
            dma((2,)),
            dma((2,)),
            dma,
            dma((2, 2)),
            dma((2, 2, parts)),
            dma((2,)),
            dma,
            dma((parts,)),
            dma((parts,)),
            dma((2,)),
            dma((parts, TILES)),
            dma,
            dma,
        ],
        compiler_params=pltpu.CompilerParams(
            collective_id=0, has_side_effects=True, vmem_limit_bytes=62 << 20
        ),
        name="response",
    )(three_centre[0], green_occupied[0], green_virtual[0], block_sizes, screening.T)


def solution(mesh):
    return jax.shard_map(
        per_device,
        mesh=mesh,
        in_specs=(
            P("ctr", None, None, "blk", None),
            P("ctr", None, None, None),
            P("ctr", None, None, None),
            P(),
            P(),
        ),
        out_specs=P(("blk", "ctr"), None),
        check_vma=False,
    )
```

```python
import functools
import math

import jax
import jax.numpy as jnp
from jax import lax
from jax.experimental import pallas as pl
from jax.experimental.pallas import tpu as pltpu
from jax.sharding import PartitionSpec as P

MESH = pl.DeviceIdType.MESH
SIDE = 4
ROWS = 16
TILES = 4
LANES = 128
AT_ONCE = 4

PLANE = (
    (2, 2), (1, 2), (3, 2), (2, 1), (2, 3),
    (0, 2), (2, 0), (1, 1), (3, 3), (1, 3), (3, 1),
    (0, 1), (0, 3), (1, 0), (3, 0),
)


def mm(a, b):
    return jnp.dot(a, b, preferred_element_type=jnp.float32)


def mm_nt(a, b):
    return lax.dot_general(a, b, (((1,), (1,)), ((), ())), preferred_element_type=jnp.float32)


def kernel(
    tc, go_hbm, gv_hbm, sizes, screen, out,
    own, halo, mrecv, bsend, brecv, go, gvn, gmat, gomat, ms, bsc,
    xsend, xrecv, xsend_last, xrecv_last, ysend, yrecv,
    in_sems, own_sem, slot_sem, gv_sems, halo_sems, m_sems, b_send_sem, b_recv_sem, b_own_sem,
    x_send_sems, x_recv_sem, y_send_sem, y_recv_sem,
):
    width, band, share, _ = tc.shape
    parts = share // ROWS
    nblk = mrecv.shape[0]
    nctr = lax.axis_size("ctr")
    rows = width // nblk
    blk, ctr = lax.axis_index("blk"), lax.axis_index("ctr")
    y, z = blk // SIDE, lax.rem(blk, SIDE)

    def peer(dy, dz):
        return lax.rem(y + dy, SIDE) * SIDE + lax.rem(z + dz, SIDE)

    def atom(shift):
        return lax.rem(ctr + shift + nctr, nctr)

    def send(src, dst, send_sem, recv_sem, b, c):
        pltpu.make_async_remote_copy(
            src_ref=src, dst_ref=dst, send_sem=send_sem, recv_sem=recv_sem,
            device_id=(b, c), device_id_type=MESH,
        ).start()

    def wait(ref, sem):
        pltpu.make_async_copy(ref, ref, sem).wait()

    def own_copy(part):
        slot = lax.rem(part, 2)
        return pltpu.make_async_copy(
            tc.at[:, :, pl.ds(part * ROWS, ROWS), :], own.at[slot], own_sem.at[slot]
        )

    inputs = [
        pltpu.make_async_copy(src, dst, in_sems.at[n])
        for n, (src, dst) in enumerate(
            ((go_hbm, go), (gv_hbm, gvn.at[1]))
        )
    ]
    for copy in inputs:
        copy.start()
    own_copy(0).start()
    slot_copy = pltpu.make_async_copy(tc.at[pl.ds(blk * rows, rows)], mrecv.at[blk], slot_sem)
    slot_copy.start()

    barrier = pltpu.get_barrier_semaphore()
    for dy, dz in PLANE:
        pl.semaphore_signal(barrier, inc=1, device_id=(peer(dy, dz), ctr), device_id_type=MESH)
    for d in range(1, nctr):
        pl.semaphore_signal(barrier, inc=1, device_id=(blk, atom(d)), device_id_type=MESH)
    pl.semaphore_wait(barrier, len(PLANE) + nctr - 1)

    for slot, shift in ((0, 1), (1, -1)):
        send(
            gv_hbm, gvn.at[2 * slot], gv_sems.at[0, slot], gv_sems.at[1, slot], blk, atom(shift)
        )

    def first_sends(part, carry):
        piece = pl.ds(part * ROWS, ROWS)
        for slot, shift in ((0, 1), (1, -1)):
            send(
                tc.at[:, :, piece, :], halo.at[slot, part],
                halo_sems.at[0, slot, part], halo_sems.at[1, slot, part], blk, atom(shift),
            )
        for cut in range(2):
            some = rows // 2
            for dy, dz in PLANE:
                b = peer(dy, dz)
                send(
                    tc.at[pl.ds(b * rows + cut * some, some), :, piece, :],
                    mrecv.at[blk, pl.ds(cut * some, some), :, piece, :],
                    m_sems.at[0], m_sems.at[1], b, ctr,
                )
        return carry

    lax.fori_loop(0, parts, first_sends, 0)

    wide = 2 * band - 1
    terms = [(e, j) for e in range(wide) for j in range(band) if 0 <= e - j < band]
    r = lax.broadcasted_iota(jnp.int32, (width, width), 0)
    s = lax.broadcasted_iota(jnp.int32, (width, width), 1)
    for copy in inputs:
        copy.wait()
    for n, (e, j) in enumerate(terms):
        k = e - j
        keep = (r < sizes[atom(0)]) & (s < sizes[atom(j - 1)])
        if k != 1:
            keep = keep & (screen[k, atom(j - 1)] == 1)
        gomat[:, n * width : (n + 1) * width] = jnp.where(keep, go[j], jnp.zeros_like(go[j]))
    for slot in range(2):
        wait(gvn.at[2 * slot], gv_sems.at[1, slot])

    for e in range(wide):
        for o in range(band):
            here = (pl.ds(e * width, width), pl.ds(o * width, width))
            if not 0 <= e - o < band:
                gmat[here] = jnp.zeros((width, width), gmat.dtype)
                continue
            keep = (r < sizes[atom(e - 2)]) & (s < sizes[atom(o - 1)])
            if o != 1:
                keep = keep & (screen[o, atom(0)] == 1)
            gmat[here] = jnp.where(keep, gvn[o, e - o], jnp.zeros((width, width), gmat.dtype))

    def second_sends(part):
        for cut in range(2):
            some = pl.ds(cut * (rows // 2), rows // 2)
            for dy, dz in PLANE:
                b = peer(dy, dz)
                send(
                    bsend.at[part, b, some], brecv.at[part, blk, some],
                    b_send_sem, b_recv_sem.at[part], b, ctr,
                )
        pltpu.make_async_copy(bsend.at[part, blk], brecv.at[part, blk], b_own_sem.at[part]).start()

    def transform(part, carry):
        slot = lax.rem(part, 2)
        own_copy(part).wait()

        @pl.when(part + 1 < parts)
        def _():
            own_copy(part + 1).start()

        step = 16
        for j in (1, 0, 2):
            if j != 1:
                wait(halo.at[j // 2, part], halo_sems.at[1, j // 2, part])

            def columns(t, carry):
                at = pl.ds(t * step, step)
                x = own[slot, at] if j == 1 else halo[j // 2, part, at]
                for k in range(band):
                    y = x[:, k].reshape(step * ROWS, width).astype(jnp.float32)
                    ms[j, k, pl.ds(t * step * ROWS, step * ROWS), :] = y
                return carry

            lax.fori_loop(0, width // step, columns, 0)

        def green(g, carry):
            places = [pl.ds(g * AT_ONCE + p, width, stride=ROWS) for p in range(AT_ONCE)]
            half = []
            for e in range(wide):
                js = [n for n, (of, _) in enumerate(terms) if of == e]
                right = jnp.concatenate(
                    [
                        jnp.concatenate(
                            [
                                ms[terms[n][1], e - terms[n][1], at, :].astype(jnp.bfloat16)
                                for at in places
                            ],
                            axis=1,
                        )
                        for n in js
                    ],
                    axis=0,
                )
                left = gomat[:, js[0] * width : (js[-1] + 1) * width]
                half.append(mm(left, right).astype(jnp.bfloat16))
            left = jnp.concatenate(
                [
                    jnp.concatenate([h[:, p * width : (p + 1) * width] for h in half], axis=1)
                    for p in range(AT_ONCE)
                ],
                axis=0,
            )
            b = mm(left, gmat[...])
            for p, at in enumerate(places):
                for o in range(band):
                    bsc[o, at, :] = b[p * width : (p + 1) * width, o * width : (o + 1) * width]
            return carry

        lax.fori_loop(0, ROWS // AT_ONCE, green, 0)

        def rounded(i, carry):
            for o in range(band):
                b = bsc[o, pl.ds(i * rows * ROWS, rows * ROWS), :].astype(jnp.bfloat16)
                bsend[part, i, :, o] = b.reshape(rows, ROWS, width)
            return carry

        lax.fori_loop(0, nblk, rounded, 0)

        @pl.when(part > 0)
        def _():
            second_sends(part - 1)

        return carry

    lax.fori_loop(0, parts, transform, 0)

    slot_copy.wait()
    wait(mrecv.at[pl.ds(0, nblk - 1)], m_sems.at[1])

    group = nblk // TILES
    cols = nblk * ROWS
    last = parts - 1

    def first(t):
        return lax.rem(y + t, TILES) * group

    def product(part, sent, got, send_sem):
        pltpu.make_async_copy(bsend.at[part, blk], brecv.at[part, blk], b_own_sem.at[part]).wait()
        wait(brecv.at[part, pl.ds(0, nblk - 1)], b_recv_sem.at[part])

        def tile(t, carry):
            at = pl.ds(first(t), group)
            here = pl.ds(pl.multiple_of(t * group * 8, group * 8), group * 8)
            acc = None
            for m0 in range(0, rows, 2):
                pairs = [(m, o) for m in (m0, m0 + 1) for o in range(band)]
                left = jnp.concatenate(
                    [mrecv[at, m, o].reshape(group * share, width) for m, o in pairs], axis=1
                )
                right = jnp.concatenate(
                    [brecv[part, :, m, o].reshape(cols, width) for m, o in pairs], axis=1
                )
                term = mm_nt(left, right)
                acc = term if acc is None else acc + term
            acc = acc.reshape(group, nctr, 8, cols)
            for c in range(nctr):
                sent[c, here, :] = acc[:, c].reshape(group * 8, cols).astype(sent.dtype)
            for d in range(1, nctr):
                c = atom(d)
                send(
                    sent.at[c, here, :], got.at[d - 1, here, :],
                    send_sem, x_recv_sem.at[part, t], blk, c,
                )
            return carry

        lax.fori_loop(0, TILES, tile, 0)

    def reduce(part, sent, got):
        def tile(t, carry):
            here = pl.ds(pl.multiple_of(t * group * 8, group * 8), group * 8)
            wait(got.at[:, here, :], x_recv_sem.at[part, t])
            total = sent[ctr, here, :].astype(jnp.float32)
            for d in range(nctr - 1):
                total = total + got[d, here, :].astype(jnp.float32)
            ysend[part, here, :] = total
            for i in range(group):
                b = first(t) + i
                row = pl.ds(pl.multiple_of((t * group + i) * 8, 8), 8)

                @pl.when(b == blk)
                def _():
                    yrecv[part, blk] = ysend[part, row, :]

                @pl.when(b != blk)
                def _():
                    send(ysend.at[part, row, :], yrecv.at[part, blk], y_send_sem, y_recv_sem, b, ctr)

            return carry

        lax.fori_loop(0, TILES, tile, 0)

    def middle(part, carry):
        product(part, xsend.at[part], xrecv.at[part], x_send_sems.at[0])

        @pl.when(part == 1)
        def _():
            second_sends(last)

        @pl.when(part > 0)
        def _():
            reduce(part - 1, xsend.at[part - 1], xrecv.at[part - 1])

        return carry

    lax.fori_loop(0, last, middle, 0)
    product(last, xsend_last, xrecv_last, x_send_sems.at[1])
    reduce(last - 1, xsend.at[last - 1], xrecv.at[last - 1])
    reduce(last, xsend_last, xrecv_last)

    scale = -2.0 / (width * math.sqrt(nctr * band))
    wait(yrecv.at[:, pl.ds(0, nblk - 1)], y_recv_sem)
    lane = lax.broadcasted_iota(jnp.int32, (8, LANES), 1)
    held = [jnp.zeros((8, LANES), jnp.float32) for _ in range(nblk * share // LANES)]
    for part in range(parts):
        total = yrecv[part, 0]
        for n in range(1, nblk):
            total = total + yrecv[part, n]
        total = total * scale
        for n in range(nblk):
            at, to = n * ROWS, n * share + part * ROWS
            piece = total[:, at // LANES * LANES : (at // LANES + 1) * LANES]
            shift = (to - at) % LANES
            if shift:
                piece = pltpu.roll(piece, shift, 1)
            here = (lane >= to % LANES) & (lane < to % LANES + ROWS)
            held[to // LANES] = jnp.where(here, piece, held[to // LANES])
    for n, piece in enumerate(held):
        out[:, n * LANES : (n + 1) * LANES] = piece

    for slot in range(2):
        wait(gvn.at[2 * slot], gv_sems.at[0, slot])
        for part in range(parts):
            wait(halo.at[slot, part], halo_sems.at[0, slot, part])
    wait(mrecv.at[pl.ds(0, nblk - 1)], m_sems.at[0])
    wait(brecv.at[:, pl.ds(0, nblk - 1)], b_send_sem)
    wait(xrecv, x_send_sems.at[0])
    wait(xrecv_last, x_send_sems.at[1])
    wait(yrecv.at[:, pl.ds(0, nblk - 1)], y_send_sem)


def packed_kernel(
    tc, go_hbm, gv_hbm, sizes, screen, out,
    own, halo, msend, mrecv, bsend, brecv, go, gvn, gmat, gomat, sel, pgmat, ms, bsc,
    xsend, xrecv, xsend_last, xrecv_last, ysend, yrecv,
    in_sems, own_sem, slot_sem, gv_sems, halo_sems, m_sems, b_send_sem, b_recv_sem, b_own_sem,
    x_send_sems, x_recv_sem, y_send_sem, y_recv_sem,
):
    width, band, share, _ = tc.shape
    parts = share // ROWS
    nblk = mrecv.shape[0]
    nctr = lax.axis_size("ctr")
    rows = width // nblk
    blk, ctr = lax.axis_index("blk"), lax.axis_index("ctr")
    y, z = blk // SIDE, lax.rem(blk, SIDE)

    def peer(dy, dz):
        return lax.rem(y + dy, SIDE) * SIDE + lax.rem(z + dz, SIDE)

    def atom(shift):
        return lax.rem(ctr + shift + nctr, nctr)

    def send(src, dst, send_sem, recv_sem, b, c):
        pltpu.make_async_remote_copy(
            src_ref=src, dst_ref=dst, send_sem=send_sem, recv_sem=recv_sem,
            device_id=(b, c), device_id_type=MESH,
        ).start()

    def wait(ref, sem):
        pltpu.make_async_copy(ref, ref, sem).wait()

    def own_copy(part):
        slot = lax.rem(part, 2)
        return pltpu.make_async_copy(
            tc.at[:, :, pl.ds(part * ROWS, ROWS), :], own.at[slot], own_sem.at[slot]
        )

    inputs = [
        pltpu.make_async_copy(src, dst, in_sems.at[n])
        for n, (src, dst) in enumerate(
            ((go_hbm, go), (gv_hbm, gvn.at[1]))
        )
    ]
    for copy in inputs:
        copy.start()
    own_copy(0).start()
    barrier = pltpu.get_barrier_semaphore()
    for dy, dz in PLANE:
        pl.semaphore_signal(barrier, inc=1, device_id=(peer(dy, dz), ctr), device_id_type=MESH)
    for d in range(1, nctr):
        pl.semaphore_signal(barrier, inc=1, device_id=(blk, atom(d)), device_id_type=MESH)

    at = jnp.int32(0)
    r = lax.broadcasted_iota(jnp.int32, (width, band * width), 0)
    s = lax.broadcasted_iota(jnp.int32, (width, band * width), 1)
    for o in range(band):
        length = sizes[atom(o - 1)]
        if o != 1:
            length = jnp.where(screen[o, atom(0)] == 1, length, 0)
        for i in range(2):
            here = (s - r == at + i * (width // 2)) & (r < length)
            sel[i, o * width : (o + 1) * width, :] = jnp.where(here, 1.0, 0.0).astype(sel.dtype)
        at = at + length

    def fold(even, odd):
        cut = lambda v: [v[:, n * width : (n + 1) * width] for n in range(band)]
        even, odd = cut(even), cut(odd)
        return [*even[:-1], even[-1] + odd[0], *odd[1:]]

    def pack(part):
        slot = lax.rem(part, 2)
        own_copy(part).wait()

        @pl.when(part + 1 < parts)
        def _():
            own_copy(part + 1).start()

        def some(g, carry):
            x = own[slot, pl.ds(g * 4 * rows, 4 * rows)]
            x = x.reshape(2 * rows, 2, band, ROWS, width)
            even, odd = (
                jnp.concatenate(
                    [x[:, i, n].reshape(2 * rows * ROWS, width) for n in range(band)], axis=1
                )
                for i in range(2)
            )
            for t, v in enumerate(fold(mm(even, sel[0]), mm(odd, sel[1]))):
                msend[part, pl.ds(g * 4, 4), :, t] = v.astype(jnp.bfloat16).reshape(
                    4, rows // 2, ROWS, width
                )
            return carry

        lax.fori_loop(0, nblk // 4, some, 0)

    pack(jnp.int32(0))
    pl.semaphore_wait(barrier, len(PLANE) + nctr - 1)

    for slot, shift in ((0, 1), (1, -1)):
        send(
            gv_hbm, gvn.at[2 * slot], gv_sems.at[0, slot], gv_sems.at[1, slot], blk, atom(shift)
        )

    def first_sends(part, carry):
        piece = pl.ds(part * ROWS, ROWS)
        for slot, shift in ((0, 1), (1, -1)):
            send(
                tc.at[:, :, piece, :], halo.at[slot, part],
                halo_sems.at[0, slot, part], halo_sems.at[1, slot, part], blk, atom(shift),
            )

        @pl.when(part > 0)
        def _():
            pack(part)

        for cut in range(2):
            some = pl.ds(cut * (rows // 4), rows // 4)
            for dy, dz in PLANE:
                b = peer(dy, dz)
                send(
                    msend.at[part, b, some], mrecv.at[blk, some, :, piece, :],
                    m_sems.at[0], m_sems.at[1], b, ctr,
                )
        pltpu.make_async_copy(
            msend.at[part, blk], mrecv.at[blk, :, :, piece, :], slot_sem
        ).start()
        return carry

    lax.fori_loop(0, parts, first_sends, 0)
    own_copy(0).start()

    wide = 2 * band - 1
    terms = [(e, j) for e in range(wide) for j in range(band) if 0 <= e - j < band]
    r = lax.broadcasted_iota(jnp.int32, (width, width), 0)
    s = lax.broadcasted_iota(jnp.int32, (width, width), 1)
    for copy in inputs:
        copy.wait()
    half_width = width // 2
    place = jnp.where(r < half_width, 2 * r, 2 * (r - half_width) + 1)
    order = jnp.where(s == place, 1.0, 0.0).astype(jnp.bfloat16)
    for n, (e, j) in enumerate(terms):
        k = e - j
        keep = (r < sizes[atom(0)]) & (s < sizes[atom(j - 1)])
        if k != 1:
            keep = keep & (screen[k, atom(j - 1)] == 1)
        block = jnp.where(keep, go[j], jnp.zeros_like(go[j]))
        gomat[:, n * width : (n + 1) * width] = mm(order, block).astype(gomat.dtype)
    for slot in range(2):
        wait(gvn.at[2 * slot], gv_sems.at[1, slot])

    for e in range(wide):
        for o in range(band):
            here = (pl.ds(e * width, width), pl.ds(o * width, width))
            if not 0 <= e - o < band:
                gmat[here] = jnp.zeros((width, width), gmat.dtype)
                continue
            keep = (r < sizes[atom(e - 2)]) & (s < sizes[atom(o - 1)])
            if o != 1:
                keep = keep & (screen[o, atom(0)] == 1)
            gmat[here] = jnp.where(keep, gvn[o, e - o], jnp.zeros((width, width), gmat.dtype))

    def second_sends(part):
        for cut in range(2):
            some = pl.ds(cut * (rows // 4), rows // 4)
            for dy, dz in PLANE:
                b = peer(dy, dz)
                send(
                    bsend.at[part, b, some], brecv.at[part, blk, some],
                    b_send_sem, b_recv_sem.at[part], b, ctr,
                )
        pltpu.make_async_copy(bsend.at[part, blk], brecv.at[part, blk], b_own_sem.at[part]).start()

    for i in range(2):
        pgmat[i] = mm(gmat[...], sel[i]).astype(pgmat.dtype)

    def transform(part, carry):
        slot = lax.rem(part, 2)
        own_copy(part).wait()

        @pl.when(part + 1 < parts)
        def _():
            own_copy(part + 1).start()

        step = 16
        for j in (1, 0, 2):
            if j != 1:
                wait(halo.at[j // 2, part], halo_sems.at[1, j // 2, part])

            def columns(t, carry):
                at = pl.ds(t * step, step)
                x = own[slot, at] if j == 1 else halo[j // 2, part, at]
                for k in range(band):
                    y = x[:, k].reshape(step * ROWS, width).astype(jnp.float32)
                    ms[j, k, pl.ds(t * step * ROWS, step * ROWS), :] = y
                return carry

            lax.fori_loop(0, width // step, columns, 0)

        def green(g, carry):
            places = [pl.ds(g * AT_ONCE + p, width, stride=ROWS) for p in range(AT_ONCE)]
            half = []
            for e in range(wide):
                js = [n for n, (of, _) in enumerate(terms) if of == e]
                right = jnp.concatenate(
                    [
                        jnp.concatenate(
                            [
                                ms[terms[n][1], e - terms[n][1], at, :].astype(jnp.bfloat16)
                                for at in places
                            ],
                            axis=1,
                        )
                        for n in js
                    ],
                    axis=0,
                )
                left = gomat[:, js[0] * width : (js[-1] + 1) * width]
                half.append(mm(left, right).astype(jnp.bfloat16))
            both = []
            for i in range(2):
                left = jnp.concatenate(
                    [
                        jnp.concatenate(
                            [
                                h[
                                    i * half_width : (i + 1) * half_width,
                                    p * width : (p + 1) * width,
                                ]
                                for h in half
                            ],
                            axis=1,
                        )
                        for p in range(AT_ONCE)
                    ],
                    axis=0,
                )
                both.append(mm(left, pgmat[i]))
            for t, v in enumerate(fold(*both)):
                for p in range(AT_ONCE):
                    at = pl.ds(g * AT_ONCE + p, half_width, stride=ROWS)
                    bsc[t, at, :] = v[p * half_width : (p + 1) * half_width]
            return carry

        lax.fori_loop(0, ROWS // AT_ONCE, green, 0)

        def rounded(i, carry):
            some = rows // 2
            for t in range(2 * band - 1):
                b = bsc[t, pl.ds(i * some * ROWS, some * ROWS), :].astype(jnp.bfloat16)
                bsend[part, i, :, t] = b.reshape(some, ROWS, width)
            return carry

        lax.fori_loop(0, nblk, rounded, 0)

        @pl.when(part > 0)
        def _():
            second_sends(part - 1)

        return carry

    lax.fori_loop(0, parts, transform, 0)

    wait(mrecv.at[blk], slot_sem)
    wait(mrecv.at[pl.ds(0, nblk - 1)], m_sems.at[1])

    group = nblk // TILES
    cols = nblk * ROWS
    last = parts - 1

    def first(t):
        return lax.rem(y + t, TILES) * group

    def product(part, sent, got, send_sem):
        pltpu.make_async_copy(bsend.at[part, blk], brecv.at[part, blk], b_own_sem.at[part]).wait()
        wait(brecv.at[part, pl.ds(0, nblk - 1)], b_recv_sem.at[part])

        def tile(t, carry):
            at = pl.ds(first(t), group)
            here = pl.ds(pl.multiple_of(t * group * 8, group * 8), group * 8)
            acc = None
            for m0 in range(0, rows // 2, 2):
                pairs = [(m, o) for m in (m0, m0 + 1) for o in range(2 * band - 1)]
                left = jnp.concatenate(
                    [mrecv[at, m, o].reshape(group * share, width) for m, o in pairs], axis=1
                )
                right = jnp.concatenate(
                    [brecv[part, :, m, o].reshape(cols, width) for m, o in pairs], axis=1
                )
                term = mm_nt(left, right)
                acc = term if acc is None else acc + term
            acc = acc.reshape(group, nctr, 8, cols)
            for c in range(nctr):
                sent[c, here, :] = acc[:, c].reshape(group * 8, cols).astype(sent.dtype)
            for d in range(1, nctr):
                c = atom(d)
                send(
                    sent.at[c, here, :], got.at[d - 1, here, :],
                    send_sem, x_recv_sem.at[part, t], blk, c,
                )
            return carry

        lax.fori_loop(0, TILES, tile, 0)

    def reduce(part, sent, got):
        def tile(t, carry):
            here = pl.ds(pl.multiple_of(t * group * 8, group * 8), group * 8)
            wait(got.at[:, here, :], x_recv_sem.at[part, t])
            total = sent[ctr, here, :].astype(jnp.float32)
            for d in range(nctr - 1):
                total = total + got[d, here, :].astype(jnp.float32)
            ysend[part, here, :] = total
            for i in range(group):
                b = first(t) + i
                row = pl.ds(pl.multiple_of((t * group + i) * 8, 8), 8)

                @pl.when(b == blk)
                def _():
                    yrecv[part, blk] = ysend[part, row, :]

                @pl.when(b != blk)
                def _():
                    send(ysend.at[part, row, :], yrecv.at[part, blk], y_send_sem, y_recv_sem, b, ctr)

            return carry

        lax.fori_loop(0, TILES, tile, 0)

    def middle(part, carry):
        product(part, xsend.at[part], xrecv.at[part], x_send_sems.at[0])

        @pl.when(part == 1)
        def _():
            second_sends(last)

        @pl.when(part > 0)
        def _():
            reduce(part - 1, xsend.at[part - 1], xrecv.at[part - 1])

        return carry

    lax.fori_loop(0, last, middle, 0)
    product(last, xsend_last, xrecv_last, x_send_sems.at[1])
    reduce(last - 1, xsend.at[last - 1], xrecv.at[last - 1])
    reduce(last, xsend_last, xrecv_last)

    scale = -2.0 / (width * math.sqrt(nctr * band))
    wait(yrecv.at[:, pl.ds(0, nblk - 1)], y_recv_sem)
    lane = lax.broadcasted_iota(jnp.int32, (8, LANES), 1)
    held = [jnp.zeros((8, LANES), jnp.float32) for _ in range(nblk * share // LANES)]
    for part in range(parts):
        total = yrecv[part, 0]
        for n in range(1, nblk):
            total = total + yrecv[part, n]
        total = total * scale
        for n in range(nblk):
            at, to = n * ROWS, n * share + part * ROWS
            piece = total[:, at // LANES * LANES : (at // LANES + 1) * LANES]
            shift = (to - at) % LANES
            if shift:
                piece = pltpu.roll(piece, shift, 1)
            here = (lane >= to % LANES) & (lane < to % LANES + ROWS)
            held[to // LANES] = jnp.where(here, piece, held[to // LANES])
    for n, piece in enumerate(held):
        out[:, n * LANES : (n + 1) * LANES] = piece

    for slot in range(2):
        wait(gvn.at[2 * slot], gv_sems.at[0, slot])
        for part in range(parts):
            wait(halo.at[slot, part], halo_sems.at[0, slot, part])
    wait(mrecv.at[pl.ds(0, nblk - 1)], m_sems.at[0])
    wait(brecv.at[:, pl.ds(0, nblk - 1)], b_send_sem)
    wait(xrecv, x_send_sems.at[0])
    wait(xrecv_last, x_send_sems.at[1])
    wait(yrecv.at[:, pl.ds(0, nblk - 1)], y_send_sem)


def run(packed, three_centre, green_occupied, green_virtual, block_sizes, screening):
    _, width, band, share, _ = three_centre.shape
    nblk, nctr = lax.axis_size("blk"), lax.axis_size("ctr")
    parts, rows, cols = share // ROWS, width // nblk, nblk * ROWS
    bf16, f32 = jnp.bfloat16, jnp.float32
    vmem, dma = pltpu.VMEM, pltpu.SemaphoreType.DMA
    units, tiles = (rows // 2, 2 * band - 1) if packed else (rows, band)
    one = lambda *a: [vmem(*a)] if packed else []
    return pl.pallas_call(
        packed_kernel if packed else kernel,
        out_shape=jax.ShapeDtypeStruct((8, nblk * share), f32),
        in_specs=[
            pl.BlockSpec(memory_space=pl.ANY),
            pl.BlockSpec(memory_space=pl.ANY),
            pl.BlockSpec(memory_space=pl.ANY),
            pl.BlockSpec(memory_space=pltpu.SMEM),
            pl.BlockSpec(memory_space=pltpu.SMEM),
        ],
        out_specs=pl.BlockSpec(memory_space=pltpu.VMEM),
        scratch_shapes=[
            vmem((2, width, band, ROWS, width), bf16),
            vmem((2, parts, width, band, ROWS, width), bf16),
            *one((parts, nblk, units, tiles, ROWS, width), bf16),
            vmem((nblk, units, tiles, share, width), bf16),
            vmem((parts, nblk, units, tiles, ROWS, width), bf16),
            vmem((parts, nblk, units, tiles, ROWS, width), bf16),
            vmem((band, width, width), bf16),
            vmem((3, band, width, width), bf16),
            vmem(((2 * band - 1) * width, band * width), bf16),
            vmem((width, band * band * width), bf16),
            *one((2, band * width, band * width), bf16),
            *one((2, (2 * band - 1) * width, band * width), bf16),
            vmem((band, band, width * ROWS, width), f32),
            vmem((tiles, width * ROWS * units // rows, width), f32),
            vmem((parts - 1, nctr, nblk * 8, cols), f32),
            vmem((parts - 1, nctr - 1, nblk * 8, cols), f32),
            vmem((nctr, nblk * 8, cols), bf16),
            vmem((nctr - 1, nblk * 8, cols), bf16),
            vmem((parts, nblk * 8, cols), f32),
            vmem((parts, nblk, 8, cols), f32),
            dma((2,)),
            dma((2,)),
            dma,
            dma((2, 2)),
            dma((2, 2, parts)),
            dma((2,)),
            dma,
            dma((parts,)),
            dma((parts,)),
            dma((2,)),
            dma((parts, TILES)),
            dma,
            dma,
        ],
        compiler_params=pltpu.CompilerParams(
            collective_id=int(packed), has_side_effects=True, vmem_limit_bytes=62 << 20
        ),
        name="response_packed" if packed else "response",
    )(three_centre[0], green_occupied[0], green_virtual[0], block_sizes, screening.T)


def per_device(*args):
    sizes, screen = args[3], args[4]
    band = screen.shape[1]
    cols = sum(
        jnp.where((screen[:, k] == 1) | (k == band // 2), jnp.roll(sizes, band // 2 - k), 0)
        for k in range(band)
    )
    fits = jnp.max(cols) <= (2 * band - 1) * args[0].shape[1] // 2
    return lax.cond(fits, functools.partial(run, True), functools.partial(run, False), *args)


def solution(mesh):
    return jax.shard_map(
        per_device,
        mesh=mesh,
        in_specs=(
            P("ctr", None, None, "blk", None),
            P("ctr", None, None, None),
            P("ctr", None, None, None),
            P(),
            P(),
        ),
        out_specs=P(("blk", "ctr"), None),
        check_vma=False,
    )
```

```python
import functools
import math

import jax
import jax.numpy as jnp
from jax import lax
from jax.experimental import pallas as pl
from jax.experimental.pallas import tpu as pltpu
from jax.sharding import PartitionSpec as P

MESH = pl.DeviceIdType.MESH
SIDE = 4
ROWS = 16
TILES = 4
LANES = 128
AT_ONCE = 4

PLANE = (
    (2, 2), (1, 2), (3, 2), (2, 1), (2, 3),
    (0, 2), (2, 0), (1, 1), (3, 3), (1, 3), (3, 1),
    (0, 1), (0, 3), (1, 0), (3, 0),
)


def mm(a, b):
    return jnp.dot(a, b, preferred_element_type=jnp.float32)


def mm_nt(a, b):
    return lax.dot_general(a, b, (((1,), (1,)), ((), ())), preferred_element_type=jnp.float32)


def kernel(
    tc, go_hbm, gv_hbm, sizes, screen, out,
    own, halo, mrecv, bsend, brecv, go, gvn, gmat, gomat, ms, bsc,
    xsend, xrecv, xsend_last, xrecv_last, ysend, yrecv,
    in_sems, own_sem, slot_sem, gv_sems, halo_sems, m_sems, b_send_sem, b_recv_sem, b_own_sem,
    x_send_sems, x_recv_sem, y_send_sem, y_recv_sem,
):
    width, band, share, _ = tc.shape
    parts = share // ROWS
    nblk = mrecv.shape[0]
    nctr = lax.axis_size("ctr")
    rows = width // nblk
    blk, ctr = lax.axis_index("blk"), lax.axis_index("ctr")
    y, z = blk // SIDE, lax.rem(blk, SIDE)

    def peer(dy, dz):
        return lax.rem(y + dy, SIDE) * SIDE + lax.rem(z + dz, SIDE)

    def atom(shift):
        return lax.rem(ctr + shift + nctr, nctr)

    def send(src, dst, send_sem, recv_sem, b, c):
        pltpu.make_async_remote_copy(
            src_ref=src, dst_ref=dst, send_sem=send_sem, recv_sem=recv_sem,
            device_id=(b, c), device_id_type=MESH,
        ).start()

    def wait(ref, sem):
        pltpu.make_async_copy(ref, ref, sem).wait()

    def own_copy(part):
        slot = lax.rem(part, 2)
        return pltpu.make_async_copy(
            tc.at[:, :, pl.ds(part * ROWS, ROWS), :], own.at[slot], own_sem.at[slot]
        )

    inputs = [
        pltpu.make_async_copy(src, dst, in_sems.at[n])
        for n, (src, dst) in enumerate(
            ((go_hbm, go), (gv_hbm, gvn.at[1]))
        )
    ]
    for copy in inputs:
        copy.start()
    own_copy(0).start()
    slot_copy = pltpu.make_async_copy(tc.at[pl.ds(blk * rows, rows)], mrecv.at[blk], slot_sem)
    slot_copy.start()

    barrier = pltpu.get_barrier_semaphore()
    for dy, dz in PLANE:
        pl.semaphore_signal(barrier, inc=1, device_id=(peer(dy, dz), ctr), device_id_type=MESH)
    for d in range(1, nctr):
        pl.semaphore_signal(barrier, inc=1, device_id=(blk, atom(d)), device_id_type=MESH)
    pl.semaphore_wait(barrier, len(PLANE) + nctr - 1)

    for slot, shift in ((0, 1), (1, -1)):
        send(
            gv_hbm, gvn.at[2 * slot], gv_sems.at[0, slot], gv_sems.at[1, slot], blk, atom(shift)
        )

    def first_sends(part, carry):
        piece = pl.ds(part * ROWS, ROWS)
        for slot, shift in ((0, 1), (1, -1)):
            send(
                tc.at[:, :, piece, :], halo.at[slot, part],
                halo_sems.at[0, slot, part], halo_sems.at[1, slot, part], blk, atom(shift),
            )
        for cut in range(2):
            some = rows // 2
            for dy, dz in PLANE:
                b = peer(dy, dz)
                send(
                    tc.at[pl.ds(b * rows + cut * some, some), :, piece, :],
                    mrecv.at[blk, pl.ds(cut * some, some), :, piece, :],
                    m_sems.at[0], m_sems.at[1], b, ctr,
                )
        return carry

    lax.fori_loop(0, parts, first_sends, 0)

    wide = 2 * band - 1
    terms = [(e, j) for e in range(wide) for j in range(band) if 0 <= e - j < band]
    r = lax.broadcasted_iota(jnp.int32, (width, width), 0)
    s = lax.broadcasted_iota(jnp.int32, (width, width), 1)
    for copy in inputs:
        copy.wait()
    for n, (e, j) in enumerate(terms):
        k = e - j
        keep = (r < sizes[atom(0)]) & (s < sizes[atom(j - 1)])
        if k != 1:
            keep = keep & (screen[k, atom(j - 1)] == 1)
        gomat[:, n * width : (n + 1) * width] = jnp.where(keep, go[j], jnp.zeros_like(go[j]))
    for slot in range(2):
        wait(gvn.at[2 * slot], gv_sems.at[1, slot])

    for e in range(wide):
        for o in range(band):
            here = (pl.ds(e * width, width), pl.ds(o * width, width))
            if not 0 <= e - o < band:
                gmat[here] = jnp.zeros((width, width), gmat.dtype)
                continue
            keep = (r < sizes[atom(e - 2)]) & (s < sizes[atom(o - 1)])
            if o != 1:
                keep = keep & (screen[o, atom(0)] == 1)
            gmat[here] = jnp.where(keep, gvn[o, e - o], jnp.zeros((width, width), gmat.dtype))

    def second_sends(part):
        for cut in range(2):
            some = pl.ds(cut * (rows // 2), rows // 2)
            for dy, dz in PLANE:
                b = peer(dy, dz)
                send(
                    bsend.at[part, b, some], brecv.at[part, blk, some],
                    b_send_sem, b_recv_sem.at[part], b, ctr,
                )
        pltpu.make_async_copy(bsend.at[part, blk], brecv.at[part, blk], b_own_sem.at[part]).start()

    def transform(part, carry):
        slot = lax.rem(part, 2)
        own_copy(part).wait()

        @pl.when(part + 1 < parts)
        def _():
            own_copy(part + 1).start()

        step = 16
        for j in (1, 0, 2):
            if j != 1:
                wait(halo.at[j // 2, part], halo_sems.at[1, j // 2, part])

            def columns(t, carry):
                at = pl.ds(t * step, step)
                x = own[slot, at] if j == 1 else halo[j // 2, part, at]
                for k in range(band):
                    y = x[:, k].reshape(step * ROWS, width).astype(jnp.float32)
                    ms[j, k, pl.ds(t * step * ROWS, step * ROWS), :] = y
                return carry

            lax.fori_loop(0, width // step, columns, 0)

        def green(g, carry):
            places = [pl.ds(g * AT_ONCE + p, width, stride=ROWS) for p in range(AT_ONCE)]
            half = []
            for e in range(wide):
                js = [n for n, (of, _) in enumerate(terms) if of == e]
                right = jnp.concatenate(
                    [
                        jnp.concatenate(
                            [
                                ms[terms[n][1], e - terms[n][1], at, :].astype(jnp.bfloat16)
                                for at in places
                            ],
                            axis=1,
                        )
                        for n in js
                    ],
                    axis=0,
                )
                left = gomat[:, js[0] * width : (js[-1] + 1) * width]
                half.append(mm(left, right).astype(jnp.bfloat16))
            left = jnp.concatenate(
                [
                    jnp.concatenate([h[:, p * width : (p + 1) * width] for h in half], axis=1)
                    for p in range(AT_ONCE)
                ],
                axis=0,
            )
            b = mm(left, gmat[...])
            for p, at in enumerate(places):
                for o in range(band):
                    bsc[o, at, :] = b[p * width : (p + 1) * width, o * width : (o + 1) * width]
            return carry

        lax.fori_loop(0, ROWS // AT_ONCE, green, 0)

        def rounded(i, carry):
            for o in range(band):
                b = bsc[o, pl.ds(i * rows * ROWS, rows * ROWS), :].astype(jnp.bfloat16)
                bsend[part, i, :, o] = b.reshape(rows, ROWS, width)
            return carry

        lax.fori_loop(0, nblk, rounded, 0)

        @pl.when(part > 0)
        def _():
            second_sends(part - 1)

        return carry

    lax.fori_loop(0, parts, transform, 0)

    slot_copy.wait()
    wait(mrecv.at[pl.ds(0, nblk - 1)], m_sems.at[1])

    group = nblk // TILES
    cols = nblk * ROWS
    last = parts - 1

    def first(t):
        return lax.rem(y + t, TILES) * group

    def product(part, sent, got, send_sem):
        pltpu.make_async_copy(bsend.at[part, blk], brecv.at[part, blk], b_own_sem.at[part]).wait()
        wait(brecv.at[part, pl.ds(0, nblk - 1)], b_recv_sem.at[part])

        def tile(t, carry):
            at = pl.ds(first(t), group)
            here = pl.ds(pl.multiple_of(t * group * 8, group * 8), group * 8)
            acc = None
            for m0 in range(0, rows, 2):
                pairs = [(m, o) for m in (m0, m0 + 1) for o in range(band)]
                left = jnp.concatenate(
                    [mrecv[at, m, o].reshape(group * share, width) for m, o in pairs], axis=1
                )
                right = jnp.concatenate(
                    [brecv[part, :, m, o].reshape(cols, width) for m, o in pairs], axis=1
                )
                term = mm_nt(left, right)
                acc = term if acc is None else acc + term
            acc = acc.reshape(group, nctr, 8, cols)
            for c in range(nctr):
                sent[c, here, :] = acc[:, c].reshape(group * 8, cols).astype(sent.dtype)
            for d in range(1, nctr):
                c = atom(d)
                send(
                    sent.at[c, here, :], got.at[d - 1, here, :],
                    send_sem, x_recv_sem.at[part, t], blk, c,
                )
            return carry

        lax.fori_loop(0, TILES, tile, 0)

    def reduce(part, sent, got):
        def tile(t, carry):
            here = pl.ds(pl.multiple_of(t * group * 8, group * 8), group * 8)
            wait(got.at[:, here, :], x_recv_sem.at[part, t])
            total = sent[ctr, here, :].astype(jnp.float32)
            for d in range(nctr - 1):
                total = total + got[d, here, :].astype(jnp.float32)
            ysend[part, here, :] = total
            for i in range(group):
                b = first(t) + i
                row = pl.ds(pl.multiple_of((t * group + i) * 8, 8), 8)

                @pl.when(b == blk)
                def _():
                    yrecv[part, blk] = ysend[part, row, :]

                @pl.when(b != blk)
                def _():
                    send(ysend.at[part, row, :], yrecv.at[part, blk], y_send_sem, y_recv_sem, b, ctr)

            return carry

        lax.fori_loop(0, TILES, tile, 0)

    def middle(part, carry):
        product(part, xsend.at[part], xrecv.at[part], x_send_sems.at[0])

        @pl.when(part == 1)
        def _():
            second_sends(last)

        @pl.when(part > 0)
        def _():
            reduce(part - 1, xsend.at[part - 1], xrecv.at[part - 1])

        return carry

    lax.fori_loop(0, last, middle, 0)
    product(last, xsend_last, xrecv_last, x_send_sems.at[1])
    reduce(last - 1, xsend.at[last - 1], xrecv.at[last - 1])
    reduce(last, xsend_last, xrecv_last)

    scale = -2.0 / (width * math.sqrt(nctr * band))
    wait(yrecv.at[:, pl.ds(0, nblk - 1)], y_recv_sem)
    lane = lax.broadcasted_iota(jnp.int32, (8, LANES), 1)
    held = [jnp.zeros((8, LANES), jnp.float32) for _ in range(nblk * share // LANES)]
    for part in range(parts):
        total = yrecv[part, 0]
        for n in range(1, nblk):
            total = total + yrecv[part, n]
        total = total * scale
        for n in range(nblk):
            at, to = n * ROWS, n * share + part * ROWS
            piece = total[:, at // LANES * LANES : (at // LANES + 1) * LANES]
            shift = (to - at) % LANES
            if shift:
                piece = pltpu.roll(piece, shift, 1)
            here = (lane >= to % LANES) & (lane < to % LANES + ROWS)
            held[to // LANES] = jnp.where(here, piece, held[to // LANES])
    for n, piece in enumerate(held):
        out[:, n * LANES : (n + 1) * LANES] = piece

    for slot in range(2):
        wait(gvn.at[2 * slot], gv_sems.at[0, slot])
        for part in range(parts):
            wait(halo.at[slot, part], halo_sems.at[0, slot, part])
    wait(mrecv.at[pl.ds(0, nblk - 1)], m_sems.at[0])
    wait(brecv.at[:, pl.ds(0, nblk - 1)], b_send_sem)
    wait(xrecv, x_send_sems.at[0])
    wait(xrecv_last, x_send_sems.at[1])
    wait(yrecv.at[:, pl.ds(0, nblk - 1)], y_send_sem)


def most_columns(sizes, screen, out):
    atoms, band = sizes.shape[0], screen.shape[0]
    most = jnp.int32(0)
    for a in range(atoms):
        total = sizes[a]
        for k in (0, band - 1):
            total = total + jnp.where(screen[k, a] == 1, sizes[(a + k - 1) % atoms], 0)
        most = jnp.maximum(most, total)
    out[0] = most


def packed_kernel(
    tc, go_hbm, gv_hbm, sizes, screen, out,
    own, halo, msend, mrecv, bsend, brecv, go, gvn, gmat, gomat, sel, pgmat, ms, bsc,
    xsend, xrecv, xsend_last, xrecv_last, ysend, yrecv,
    in_sems, own_sem, slot_sem, gv_sems, halo_sems, m_sems, b_send_sem, b_recv_sem, b_own_sem,
    x_send_sems, x_recv_sem, y_send_sem, y_recv_sem,
):
    width, band, share, _ = tc.shape
    parts = share // ROWS
    nblk = mrecv.shape[0]
    nctr = lax.axis_size("ctr")
    rows = width // nblk
    blk, ctr = lax.axis_index("blk"), lax.axis_index("ctr")
    y, z = blk // SIDE, lax.rem(blk, SIDE)

    def peer(dy, dz):
        return lax.rem(y + dy, SIDE) * SIDE + lax.rem(z + dz, SIDE)

    def atom(shift):
        return lax.rem(ctr + shift + nctr, nctr)

    def send(src, dst, send_sem, recv_sem, b, c):
        pltpu.make_async_remote_copy(
            src_ref=src, dst_ref=dst, send_sem=send_sem, recv_sem=recv_sem,
            device_id=(b, c), device_id_type=MESH,
        ).start()

    def wait(ref, sem):
        pltpu.make_async_copy(ref, ref, sem).wait()

    def own_copy(part):
        slot = lax.rem(part, 2)
        return pltpu.make_async_copy(
            tc.at[:, :, pl.ds(part * ROWS, ROWS), :], own.at[slot], own_sem.at[slot]
        )

    inputs = [
        pltpu.make_async_copy(src, dst, in_sems.at[n])
        for n, (src, dst) in enumerate(
            ((go_hbm, go), (gv_hbm, gvn.at[1]))
        )
    ]
    for copy in inputs:
        copy.start()
    own_copy(0).start()
    barrier = pltpu.get_barrier_semaphore()
    for dy, dz in PLANE:
        pl.semaphore_signal(barrier, inc=1, device_id=(peer(dy, dz), ctr), device_id_type=MESH)
    for d in range(1, nctr):
        pl.semaphore_signal(barrier, inc=1, device_id=(blk, atom(d)), device_id_type=MESH)

    at = jnp.int32(0)
    r = lax.broadcasted_iota(jnp.int32, (width, band * width), 0)
    s = lax.broadcasted_iota(jnp.int32, (width, band * width), 1)
    for o in range(band):
        length = sizes[atom(o - 1)]
        if o != 1:
            length = jnp.where(screen[o, atom(0)] == 1, length, 0)
        for i in range(2):
            here = (s - r == at + i * (width // 2)) & (r < length)
            sel[i, o * width : (o + 1) * width, :] = jnp.where(here, 1.0, 0.0).astype(sel.dtype)
        at = at + length

    def fold(even, odd):
        cut = lambda v: [v[:, n * width : (n + 1) * width] for n in range(band)]
        even, odd = cut(even), cut(odd)
        return [*even[:-1], even[-1] + odd[0], *odd[1:]]

    def pack(part):
        slot = lax.rem(part, 2)
        own_copy(part).wait()

        @pl.when(part + 1 < parts)
        def _():
            own_copy(part + 1).start()

        def some(g, carry):
            x = own[slot, pl.ds(g * 4 * rows, 4 * rows)]
            x = x.reshape(2 * rows, 2, band, ROWS, width)
            even, odd = (
                jnp.concatenate(
                    [x[:, i, n].reshape(2 * rows * ROWS, width) for n in range(band)], axis=1
                )
                for i in range(2)
            )
            for t, v in enumerate(fold(mm(even, sel[0]), mm(odd, sel[1]))):
                msend[part, pl.ds(g * 4, 4), :, t] = v.astype(jnp.bfloat16).reshape(
                    4, rows // 2, ROWS, width
                )
            return carry

        lax.fori_loop(0, nblk // 4, some, 0)

    pack(jnp.int32(0))
    pl.semaphore_wait(barrier, len(PLANE) + nctr - 1)

    for slot, shift in ((0, 1), (1, -1)):
        send(
            gv_hbm, gvn.at[2 * slot], gv_sems.at[0, slot], gv_sems.at[1, slot], blk, atom(shift)
        )

    def first_sends(part, carry):
        piece = pl.ds(part * ROWS, ROWS)
        for slot, shift in ((0, 1), (1, -1)):
            send(
                tc.at[:, :, piece, :], halo.at[slot, part],
                halo_sems.at[0, slot, part], halo_sems.at[1, slot, part], blk, atom(shift),
            )

        @pl.when(part > 0)
        def _():
            pack(part)

        for cut in range(2):
            some = pl.ds(cut * (rows // 4), rows // 4)
            for dy, dz in PLANE:
                b = peer(dy, dz)
                send(
                    msend.at[part, b, some], mrecv.at[blk, some, :, piece, :],
                    m_sems.at[0], m_sems.at[1], b, ctr,
                )
        pltpu.make_async_copy(
            msend.at[part, blk], mrecv.at[blk, :, :, piece, :], slot_sem
        ).start()
        return carry

    lax.fori_loop(0, parts, first_sends, 0)
    own_copy(0).start()

    wide = 2 * band - 1
    terms = [(e, j) for e in range(wide) for j in range(band) if 0 <= e - j < band]
    r = lax.broadcasted_iota(jnp.int32, (width, width), 0)
    s = lax.broadcasted_iota(jnp.int32, (width, width), 1)
    for copy in inputs:
        copy.wait()
    half_width = width // 2
    place = jnp.where(r < half_width, 2 * r, 2 * (r - half_width) + 1)
    order = jnp.where(s == place, 1.0, 0.0).astype(jnp.bfloat16)
    for n, (e, j) in enumerate(terms):
        k = e - j
        keep = (r < sizes[atom(0)]) & (s < sizes[atom(j - 1)])
        if k != 1:
            keep = keep & (screen[k, atom(j - 1)] == 1)
        block = jnp.where(keep, go[j], jnp.zeros_like(go[j]))
        gomat[:, n * width : (n + 1) * width] = mm(order, block).astype(gomat.dtype)
    for slot in range(2):
        wait(gvn.at[2 * slot], gv_sems.at[1, slot])

    for e in range(wide):
        for o in range(band):
            here = (pl.ds(e * width, width), pl.ds(o * width, width))
            if not 0 <= e - o < band:
                gmat[here] = jnp.zeros((width, width), gmat.dtype)
                continue
            keep = (r < sizes[atom(e - 2)]) & (s < sizes[atom(o - 1)])
            if o != 1:
                keep = keep & (screen[o, atom(0)] == 1)
            gmat[here] = jnp.where(keep, gvn[o, e - o], jnp.zeros((width, width), gmat.dtype))

    def second_sends(part):
        for cut in range(2):
            some = pl.ds(cut * (rows // 4), rows // 4)
            for dy, dz in PLANE:
                b = peer(dy, dz)
                send(
                    bsend.at[part, b, some], brecv.at[part, blk, some],
                    b_send_sem, b_recv_sem.at[part], b, ctr,
                )
        pltpu.make_async_copy(bsend.at[part, blk], brecv.at[part, blk], b_own_sem.at[part]).start()

    for i in range(2):
        pgmat[i] = mm(gmat[...], sel[i]).astype(pgmat.dtype)

    def transform(part, carry):
        slot = lax.rem(part, 2)
        own_copy(part).wait()

        @pl.when(part + 1 < parts)
        def _():
            own_copy(part + 1).start()

        step = 16
        for j in (1, 0, 2):
            if j != 1:
                wait(halo.at[j // 2, part], halo_sems.at[1, j // 2, part])

            def columns(t, carry):
                at = pl.ds(t * step, step)
                x = own[slot, at] if j == 1 else halo[j // 2, part, at]
                for k in range(band):
                    y = x[:, k].reshape(step * ROWS, width).astype(jnp.float32)
                    ms[j, k, pl.ds(t * step * ROWS, step * ROWS), :] = y
                return carry

            lax.fori_loop(0, width // step, columns, 0)

        def green(g, carry):
            places = [pl.ds(g * AT_ONCE + p, width, stride=ROWS) for p in range(AT_ONCE)]
            half = []
            for e in range(wide):
                js = [n for n, (of, _) in enumerate(terms) if of == e]
                right = jnp.concatenate(
                    [
                        jnp.concatenate(
                            [
                                ms[terms[n][1], e - terms[n][1], at, :].astype(jnp.bfloat16)
                                for at in places
                            ],
                            axis=1,
                        )
                        for n in js
                    ],
                    axis=0,
                )
                left = gomat[:, js[0] * width : (js[-1] + 1) * width]
                half.append(mm(left, right).astype(jnp.bfloat16))
            both = []
            for i in range(2):
                left = jnp.concatenate(
                    [
                        jnp.concatenate(
                            [
                                h[
                                    i * half_width : (i + 1) * half_width,
                                    p * width : (p + 1) * width,
                                ]
                                for h in half
                            ],
                            axis=1,
                        )
                        for p in range(AT_ONCE)
                    ],
                    axis=0,
                )
                both.append(mm(left, pgmat[i]))
            for t, v in enumerate(fold(*both)):
                for p in range(AT_ONCE):
                    at = pl.ds(g * AT_ONCE + p, half_width, stride=ROWS)
                    bsc[t, at, :] = v[p * half_width : (p + 1) * half_width]
            return carry

        lax.fori_loop(0, ROWS // AT_ONCE, green, 0)

        def rounded(i, carry):
            some = rows // 2
            for t in range(2 * band - 1):
                b = bsc[t, pl.ds(i * some * ROWS, some * ROWS), :].astype(jnp.bfloat16)
                bsend[part, i, :, t] = b.reshape(some, ROWS, width)
            return carry

        lax.fori_loop(0, nblk, rounded, 0)

        @pl.when(part > 0)
        def _():
            second_sends(part - 1)

        return carry

    lax.fori_loop(0, parts, transform, 0)

    wait(mrecv.at[blk], slot_sem)
    wait(mrecv.at[pl.ds(0, nblk - 1)], m_sems.at[1])

    group = nblk // TILES
    cols = nblk * ROWS
    last = parts - 1

    def first(t):
        return lax.rem(y + t, TILES) * group

    def product(part, sent, got, send_sem):
        pltpu.make_async_copy(bsend.at[part, blk], brecv.at[part, blk], b_own_sem.at[part]).wait()
        wait(brecv.at[part, pl.ds(0, nblk - 1)], b_recv_sem.at[part])

        def tile(t, carry):
            at = pl.ds(first(t), group)
            here = pl.ds(pl.multiple_of(t * group * 8, group * 8), group * 8)
            acc = None
            for m0 in range(0, rows // 2, 2):
                pairs = [(m, o) for m in (m0, m0 + 1) for o in range(2 * band - 1)]
                left = jnp.concatenate(
                    [mrecv[at, m, o].reshape(group * share, width) for m, o in pairs], axis=1
                )
                right = jnp.concatenate(
                    [brecv[part, :, m, o].reshape(cols, width) for m, o in pairs], axis=1
                )
                term = mm_nt(left, right)
                acc = term if acc is None else acc + term
            acc = acc.reshape(group, nctr, 8, cols)
            for c in range(nctr):
                sent[c, here, :] = acc[:, c].reshape(group * 8, cols).astype(sent.dtype)
            for d in range(1, nctr):
                c = atom(d)
                send(
                    sent.at[c, here, :], got.at[d - 1, here, :],
                    send_sem, x_recv_sem.at[part, t], blk, c,
                )
            return carry

        lax.fori_loop(0, TILES, tile, 0)

    def reduce(part, sent, got):
        def tile(t, carry):
            here = pl.ds(pl.multiple_of(t * group * 8, group * 8), group * 8)
            wait(got.at[:, here, :], x_recv_sem.at[part, t])
            total = sent[ctr, here, :].astype(jnp.float32)
            for d in range(nctr - 1):
                total = total + got[d, here, :].astype(jnp.float32)
            ysend[part, here, :] = total
            for i in range(group):
                b = first(t) + i
                row = pl.ds(pl.multiple_of((t * group + i) * 8, 8), 8)

                @pl.when(b == blk)
                def _():
                    yrecv[part, blk] = ysend[part, row, :]

                @pl.when(b != blk)
                def _():
                    send(ysend.at[part, row, :], yrecv.at[part, blk], y_send_sem, y_recv_sem, b, ctr)

            return carry

        lax.fori_loop(0, TILES, tile, 0)

    def middle(part, carry):
        product(part, xsend.at[part], xrecv.at[part], x_send_sems.at[0])

        @pl.when(part == 1)
        def _():
            second_sends(last)

        @pl.when(part > 0)
        def _():
            reduce(part - 1, xsend.at[part - 1], xrecv.at[part - 1])

        return carry

    lax.fori_loop(0, last, middle, 0)
    product(last, xsend_last, xrecv_last, x_send_sems.at[1])
    reduce(last - 1, xsend.at[last - 1], xrecv.at[last - 1])
    reduce(last, xsend_last, xrecv_last)

    scale = -2.0 / (width * math.sqrt(nctr * band))
    wait(yrecv.at[:, pl.ds(0, nblk - 1)], y_recv_sem)
    lane = lax.broadcasted_iota(jnp.int32, (8, LANES), 1)
    held = [jnp.zeros((8, LANES), jnp.float32) for _ in range(nblk * share // LANES)]
    for part in range(parts):
        total = yrecv[part, 0]
        for n in range(1, nblk):
            total = total + yrecv[part, n]
        total = total * scale
        for n in range(nblk):
            at, to = n * ROWS, n * share + part * ROWS
            piece = total[:, at // LANES * LANES : (at // LANES + 1) * LANES]
            shift = (to - at) % LANES
            if shift:
                piece = pltpu.roll(piece, shift, 1)
            here = (lane >= to % LANES) & (lane < to % LANES + ROWS)
            held[to // LANES] = jnp.where(here, piece, held[to // LANES])
    for n, piece in enumerate(held):
        out[:, n * LANES : (n + 1) * LANES] = piece

    for slot in range(2):
        wait(gvn.at[2 * slot], gv_sems.at[0, slot])
        for part in range(parts):
            wait(halo.at[slot, part], halo_sems.at[0, slot, part])
    wait(mrecv.at[pl.ds(0, nblk - 1)], m_sems.at[0])
    wait(brecv.at[:, pl.ds(0, nblk - 1)], b_send_sem)
    wait(xrecv, x_send_sems.at[0])
    wait(xrecv_last, x_send_sems.at[1])
    wait(yrecv.at[:, pl.ds(0, nblk - 1)], y_send_sem)


def run(packed, three_centre, green_occupied, green_virtual, block_sizes, screening):
    _, width, band, share, _ = three_centre.shape
    nblk, nctr = lax.axis_size("blk"), lax.axis_size("ctr")
    parts, rows, cols = share // ROWS, width // nblk, nblk * ROWS
    bf16, f32 = jnp.bfloat16, jnp.float32
    vmem, dma = pltpu.VMEM, pltpu.SemaphoreType.DMA
    units, tiles = (rows // 2, 2 * band - 1) if packed else (rows, band)
    one = lambda *a: [vmem(*a)] if packed else []
    return pl.pallas_call(
        packed_kernel if packed else kernel,
        out_shape=jax.ShapeDtypeStruct((8, nblk * share), f32),
        in_specs=[
            pl.BlockSpec(memory_space=pl.ANY),
            pl.BlockSpec(memory_space=pl.ANY),
            pl.BlockSpec(memory_space=pl.ANY),
            pl.BlockSpec(memory_space=pltpu.SMEM),
            pl.BlockSpec(memory_space=pltpu.SMEM),
        ],
        out_specs=pl.BlockSpec(memory_space=pltpu.VMEM),
        scratch_shapes=[
            vmem((2, width, band, ROWS, width), bf16),
            vmem((2, parts, width, band, ROWS, width), bf16),
            *one((parts, nblk, units, tiles, ROWS, width), bf16),
            vmem((nblk, units, tiles, share, width), bf16),
            vmem((parts, nblk, units, tiles, ROWS, width), bf16),
            vmem((parts, nblk, units, tiles, ROWS, width), bf16),
            vmem((band, width, width), bf16),
            vmem((3, band, width, width), bf16),
            vmem(((2 * band - 1) * width, band * width), bf16),
            vmem((width, band * band * width), bf16),
            *one((2, band * width, band * width), bf16),
            *one((2, (2 * band - 1) * width, band * width), bf16),
            vmem((band, band, width * ROWS, width), f32),
            vmem((tiles, width * ROWS * units // rows, width), f32),
            vmem((parts - 1, nctr, nblk * 8, cols), f32),
            vmem((parts - 1, nctr - 1, nblk * 8, cols), f32),
            vmem((nctr, nblk * 8, cols), bf16),
            vmem((nctr - 1, nblk * 8, cols), bf16),
            vmem((parts, nblk * 8, cols), f32),
            vmem((parts, nblk, 8, cols), f32),
            dma((2,)),
            dma((2,)),
            dma,
            dma((2, 2)),
            dma((2, 2, parts)),
            dma((2,)),
            dma,
            dma((parts,)),
            dma((parts,)),
            dma((2,)),
            dma((parts, TILES)),
            dma,
            dma,
        ],
        compiler_params=pltpu.CompilerParams(
            collective_id=int(packed), has_side_effects=True, vmem_limit_bytes=62 << 20
        ),
        name="response_packed" if packed else "response",
    )(three_centre[0], green_occupied[0], green_virtual[0], block_sizes, screening.T)


def per_device(*args):
    sizes, screen = args[3], args[4]
    band = screen.shape[1]
    cols = pl.pallas_call(
        most_columns,
        out_shape=jax.ShapeDtypeStruct((1,), jnp.int32),
        in_specs=[pl.BlockSpec(memory_space=pltpu.SMEM)] * 2,
        out_specs=pl.BlockSpec(memory_space=pltpu.SMEM),
        name="most_columns",
    )(sizes, screen.T)
    fits = cols[0] <= (2 * band - 1) * args[0].shape[1] // 2
    return lax.cond(fits, functools.partial(run, True), functools.partial(run, False), *args)


def solution(mesh):
    return jax.shard_map(
        per_device,
        mesh=mesh,
        in_specs=(
            P("ctr", None, None, "blk", None),
            P("ctr", None, None, None),
            P("ctr", None, None, None),
            P(),
            P(),
        ),
        out_specs=P(("blk", "ctr"), None),
        check_vma=False,
    )
```

```python
import functools
import math

import jax
import jax.numpy as jnp
from jax import lax
from jax.experimental import pallas as pl
from jax.experimental.pallas import tpu as pltpu
from jax.sharding import PartitionSpec as P

MESH = pl.DeviceIdType.MESH
SIDE = 4
ROWS = 16
TILES = 4
LANES = 128
FOLDS = {2: 5, 4: 11, 1: 3}
AT_ONCE = 4

PLANE = (
    (2, 2), (1, 2), (3, 2), (2, 1), (2, 3),
    (0, 2), (2, 0), (1, 1), (3, 3), (1, 3), (3, 1),
    (0, 1), (0, 3), (1, 0), (3, 0),
)


def mm(a, b):
    return jnp.dot(a, b, preferred_element_type=jnp.float32)


def mm_nt(a, b):
    return lax.dot_general(a, b, (((1,), (1,)), ((), ())), preferred_element_type=jnp.float32)


def kernel(
    tc, go_hbm, gv_hbm, sizes, screen, out,
    own, halo, mrecv, bsend, brecv, go, gvn, gmat, gomat, ms, bsc,
    xsend, xrecv, xsend_last, xrecv_last, ysend, yrecv,
    in_sems, own_sem, slot_sem, gv_sems, halo_sems, m_sems, b_send_sem, b_recv_sem, b_own_sem,
    x_send_sems, x_recv_sem, y_send_sem, y_recv_sem,
):
    width, band, share, _ = tc.shape
    parts = share // ROWS
    nblk = mrecv.shape[0]
    nctr = lax.axis_size("ctr")
    rows = width // nblk
    blk, ctr = lax.axis_index("blk"), lax.axis_index("ctr")
    y, z = blk // SIDE, lax.rem(blk, SIDE)

    def peer(dy, dz):
        return lax.rem(y + dy, SIDE) * SIDE + lax.rem(z + dz, SIDE)

    def atom(shift):
        return lax.rem(ctr + shift + nctr, nctr)

    def send(src, dst, send_sem, recv_sem, b, c):
        pltpu.make_async_remote_copy(
            src_ref=src, dst_ref=dst, send_sem=send_sem, recv_sem=recv_sem,
            device_id=(b, c), device_id_type=MESH,
        ).start()

    def wait(ref, sem):
        pltpu.make_async_copy(ref, ref, sem).wait()

    def own_copy(part):
        slot = lax.rem(part, 2)
        return pltpu.make_async_copy(
            tc.at[:, :, pl.ds(part * ROWS, ROWS), :], own.at[slot], own_sem.at[slot]
        )

    inputs = [
        pltpu.make_async_copy(src, dst, in_sems.at[n])
        for n, (src, dst) in enumerate(
            ((go_hbm, go), (gv_hbm, gvn.at[1]))
        )
    ]
    for copy in inputs:
        copy.start()
    own_copy(0).start()
    slot_copy = pltpu.make_async_copy(tc.at[pl.ds(blk * rows, rows)], mrecv.at[blk], slot_sem)
    slot_copy.start()

    barrier = pltpu.get_barrier_semaphore()
    for dy, dz in PLANE:
        pl.semaphore_signal(barrier, inc=1, device_id=(peer(dy, dz), ctr), device_id_type=MESH)
    for d in range(1, nctr):
        pl.semaphore_signal(barrier, inc=1, device_id=(blk, atom(d)), device_id_type=MESH)
    pl.semaphore_wait(barrier, len(PLANE) + nctr - 1)

    for slot, shift in ((0, 1), (1, -1)):
        send(
            gv_hbm, gvn.at[2 * slot], gv_sems.at[0, slot], gv_sems.at[1, slot], blk, atom(shift)
        )

    def first_sends(part, carry):
        piece = pl.ds(part * ROWS, ROWS)
        for slot, shift in ((0, 1), (1, -1)):
            send(
                tc.at[:, :, piece, :], halo.at[slot, part],
                halo_sems.at[0, slot, part], halo_sems.at[1, slot, part], blk, atom(shift),
            )
        for cut in range(2):
            some = rows // 2
            for dy, dz in PLANE:
                b = peer(dy, dz)
                send(
                    tc.at[pl.ds(b * rows + cut * some, some), :, piece, :],
                    mrecv.at[blk, pl.ds(cut * some, some), :, piece, :],
                    m_sems.at[0], m_sems.at[1], b, ctr,
                )
        return carry

    lax.fori_loop(0, parts, first_sends, 0)

    wide = 2 * band - 1
    terms = [(e, j) for e in range(wide) for j in range(band) if 0 <= e - j < band]
    r = lax.broadcasted_iota(jnp.int32, (width, width), 0)
    s = lax.broadcasted_iota(jnp.int32, (width, width), 1)
    for copy in inputs:
        copy.wait()
    for n, (e, j) in enumerate(terms):
        k = e - j
        keep = (r < sizes[atom(0)]) & (s < sizes[atom(j - 1)])
        if k != 1:
            keep = keep & (screen[k, atom(j - 1)] == 1)
        gomat[:, n * width : (n + 1) * width] = jnp.where(keep, go[j], jnp.zeros_like(go[j]))
    for slot in range(2):
        wait(gvn.at[2 * slot], gv_sems.at[1, slot])

    for e in range(wide):
        for o in range(band):
            here = (pl.ds(e * width, width), pl.ds(o * width, width))
            if not 0 <= e - o < band:
                gmat[here] = jnp.zeros((width, width), gmat.dtype)
                continue
            keep = (r < sizes[atom(e - 2)]) & (s < sizes[atom(o - 1)])
            if o != 1:
                keep = keep & (screen[o, atom(0)] == 1)
            gmat[here] = jnp.where(keep, gvn[o, e - o], jnp.zeros((width, width), gmat.dtype))

    def second_sends(part):
        for cut in range(2):
            some = pl.ds(cut * (rows // 2), rows // 2)
            for dy, dz in PLANE:
                b = peer(dy, dz)
                send(
                    bsend.at[part, b, some], brecv.at[part, blk, some],
                    b_send_sem, b_recv_sem.at[part], b, ctr,
                )
        pltpu.make_async_copy(bsend.at[part, blk], brecv.at[part, blk], b_own_sem.at[part]).start()

    def transform(part, carry):
        slot = lax.rem(part, 2)
        own_copy(part).wait()

        @pl.when(part + 1 < parts)
        def _():
            own_copy(part + 1).start()

        step = 16
        for j in (1, 0, 2):
            if j != 1:
                wait(halo.at[j // 2, part], halo_sems.at[1, j // 2, part])

            def columns(t, carry):
                at = pl.ds(t * step, step)
                x = own[slot, at] if j == 1 else halo[j // 2, part, at]
                for k in range(band):
                    y = x[:, k].reshape(step * ROWS, width).astype(jnp.float32)
                    ms[j, k, pl.ds(t * step * ROWS, step * ROWS), :] = y
                return carry

            lax.fori_loop(0, width // step, columns, 0)

        def green(g, carry):
            places = [pl.ds(g * AT_ONCE + p, width, stride=ROWS) for p in range(AT_ONCE)]
            half = []
            for e in range(wide):
                js = [n for n, (of, _) in enumerate(terms) if of == e]
                right = jnp.concatenate(
                    [
                        jnp.concatenate(
                            [
                                ms[terms[n][1], e - terms[n][1], at, :].astype(jnp.bfloat16)
                                for at in places
                            ],
                            axis=1,
                        )
                        for n in js
                    ],
                    axis=0,
                )
                left = gomat[:, js[0] * width : (js[-1] + 1) * width]
                half.append(mm(left, right).astype(jnp.bfloat16))
            left = jnp.concatenate(
                [
                    jnp.concatenate([h[:, p * width : (p + 1) * width] for h in half], axis=1)
                    for p in range(AT_ONCE)
                ],
                axis=0,
            )
            b = mm(left, gmat[...])
            for p, at in enumerate(places):
                for o in range(band):
                    bsc[o, at, :] = b[p * width : (p + 1) * width, o * width : (o + 1) * width]
            return carry

        lax.fori_loop(0, ROWS // AT_ONCE, green, 0)

        def rounded(i, carry):
            for o in range(band):
                b = bsc[o, pl.ds(i * rows * ROWS, rows * ROWS), :].astype(jnp.bfloat16)
                bsend[part, i, :, o] = b.reshape(rows, ROWS, width)
            return carry

        lax.fori_loop(0, nblk, rounded, 0)

        @pl.when(part > 0)
        def _():
            second_sends(part - 1)

        return carry

    lax.fori_loop(0, parts, transform, 0)

    slot_copy.wait()
    wait(mrecv.at[pl.ds(0, nblk - 1)], m_sems.at[1])

    group = nblk // TILES
    cols = nblk * ROWS
    last = parts - 1

    def first(t):
        return lax.rem(y + t, TILES) * group

    def product(part, sent, got, send_sem):
        pltpu.make_async_copy(bsend.at[part, blk], brecv.at[part, blk], b_own_sem.at[part]).wait()
        wait(brecv.at[part, pl.ds(0, nblk - 1)], b_recv_sem.at[part])

        def tile(t, carry):
            at = pl.ds(first(t), group)
            here = pl.ds(pl.multiple_of(t * group * 8, group * 8), group * 8)
            acc = None
            for m0 in range(0, rows, 2):
                pairs = [(m, o) for m in (m0, m0 + 1) for o in range(band)]
                left = jnp.concatenate(
                    [mrecv[at, m, o].reshape(group * share, width) for m, o in pairs], axis=1
                )
                right = jnp.concatenate(
                    [brecv[part, :, m, o].reshape(cols, width) for m, o in pairs], axis=1
                )
                term = mm_nt(left, right)
                acc = term if acc is None else acc + term
            acc = acc.reshape(group, nctr, 8, cols)
            for c in range(nctr):
                sent[c, here, :] = acc[:, c].reshape(group * 8, cols).astype(sent.dtype)
            for d in range(1, nctr):
                c = atom(d)
                send(
                    sent.at[c, here, :], got.at[d - 1, here, :],
                    send_sem, x_recv_sem.at[part, t], blk, c,
                )
            return carry

        lax.fori_loop(0, TILES, tile, 0)

    def reduce(part, sent, got):
        def tile(t, carry):
            here = pl.ds(pl.multiple_of(t * group * 8, group * 8), group * 8)
            wait(got.at[:, here, :], x_recv_sem.at[part, t])
            total = sent[ctr, here, :].astype(jnp.float32)
            for d in range(nctr - 1):
                total = total + got[d, here, :].astype(jnp.float32)
            ysend[part, here, :] = total
            for i in range(group):
                b = first(t) + i
                row = pl.ds(pl.multiple_of((t * group + i) * 8, 8), 8)

                @pl.when(b == blk)
                def _():
                    yrecv[part, blk] = ysend[part, row, :]

                @pl.when(b != blk)
                def _():
                    send(ysend.at[part, row, :], yrecv.at[part, blk], y_send_sem, y_recv_sem, b, ctr)

            return carry

        lax.fori_loop(0, TILES, tile, 0)

    def middle(part, carry):
        product(part, xsend.at[part], xrecv.at[part], x_send_sems.at[0])

        @pl.when(part == 1)
        def _():
            second_sends(last)

        @pl.when(part > 0)
        def _():
            reduce(part - 1, xsend.at[part - 1], xrecv.at[part - 1])

        return carry

    lax.fori_loop(0, last, middle, 0)
    product(last, xsend_last, xrecv_last, x_send_sems.at[1])
    reduce(last - 1, xsend.at[last - 1], xrecv.at[last - 1])
    reduce(last, xsend_last, xrecv_last)

    scale = -2.0 / (width * math.sqrt(nctr * band))
    wait(yrecv.at[:, pl.ds(0, nblk - 1)], y_recv_sem)
    lane = lax.broadcasted_iota(jnp.int32, (8, LANES), 1)
    held = [jnp.zeros((8, LANES), jnp.float32) for _ in range(nblk * share // LANES)]
    for part in range(parts):
        total = yrecv[part, 0]
        for n in range(1, nblk):
            total = total + yrecv[part, n]
        total = total * scale
        for n in range(nblk):
            at, to = n * ROWS, n * share + part * ROWS
            piece = total[:, at // LANES * LANES : (at // LANES + 1) * LANES]
            shift = (to - at) % LANES
            if shift:
                piece = pltpu.roll(piece, shift, 1)
            here = (lane >= to % LANES) & (lane < to % LANES + ROWS)
            held[to // LANES] = jnp.where(here, piece, held[to // LANES])
    for n, piece in enumerate(held):
        out[:, n * LANES : (n + 1) * LANES] = piece

    for slot in range(2):
        wait(gvn.at[2 * slot], gv_sems.at[0, slot])
        for part in range(parts):
            wait(halo.at[slot, part], halo_sems.at[0, slot, part])
    wait(mrecv.at[pl.ds(0, nblk - 1)], m_sems.at[0])
    wait(brecv.at[:, pl.ds(0, nblk - 1)], b_send_sem)
    wait(xrecv, x_send_sems.at[0])
    wait(xrecv_last, x_send_sems.at[1])
    wait(yrecv.at[:, pl.ds(0, nblk - 1)], y_send_sem)


def most_columns(sizes, screen, out):
    atoms, band = sizes.shape[0], screen.shape[0]
    most = jnp.int32(0)
    for a in range(atoms):
        total = sizes[a]
        for k in (0, band - 1):
            total = total + jnp.where(screen[k, a] == 1, sizes[(a + k - 1) % atoms], 0)
        most = jnp.maximum(most, total)
    out[0] = most


def packed_kernel(
    fold_rows, tc, go_hbm, gv_hbm, sizes, screen, out,
    own, halo, msend, mrecv, bsend, brecv, go, gvn, gmat, gomat, sel, pgmat, ms, bsc,
    xsend, xrecv, xsend_last, xrecv_last, ysend, yrecv,
    in_sems, own_sem, slot_sem, gv_sems, halo_sems, m_sems, b_send_sem, b_recv_sem, b_own_sem,
    x_send_sems, x_recv_sem, y_send_sem, y_recv_sem,
):
    width, band, share, _ = tc.shape
    parts = share // ROWS
    nblk = mrecv.shape[0]
    nctr = lax.axis_size("ctr")
    rows = width // nblk
    blk, ctr = lax.axis_index("blk"), lax.axis_index("ctr")
    y, z = blk // SIDE, lax.rem(blk, SIDE)

    def peer(dy, dz):
        return lax.rem(y + dy, SIDE) * SIDE + lax.rem(z + dz, SIDE)

    def atom(shift):
        return lax.rem(ctr + shift + nctr, nctr)

    def send(src, dst, send_sem, recv_sem, b, c):
        pltpu.make_async_remote_copy(
            src_ref=src, dst_ref=dst, send_sem=send_sem, recv_sem=recv_sem,
            device_id=(b, c), device_id_type=MESH,
        ).start()

    def wait(ref, sem):
        pltpu.make_async_copy(ref, ref, sem).wait()

    def own_copy(part):
        slot = lax.rem(part, 2)
        return pltpu.make_async_copy(
            tc.at[:, :, pl.ds(part * ROWS, ROWS), :], own.at[slot], own_sem.at[slot]
        )

    inputs = [
        pltpu.make_async_copy(src, dst, in_sems.at[n])
        for n, (src, dst) in enumerate(
            ((go_hbm, go), (gv_hbm, gvn.at[1]))
        )
    ]
    for copy in inputs:
        copy.start()
    own_copy(0).start()
    barrier = pltpu.get_barrier_semaphore()
    for dy, dz in PLANE:
        pl.semaphore_signal(barrier, inc=1, device_id=(peer(dy, dz), ctr), device_id_type=MESH)
    for d in range(1, nctr):
        pl.semaphore_signal(barrier, inc=1, device_id=(blk, atom(d)), device_id_type=MESH)

    at = jnp.int32(0)
    tiles = mrecv.shape[2]
    units = rows // fold_rows
    limit = tiles * width // fold_rows
    spots = [
        (n * limit // width, n * limit % width, -(-(n * limit % width + limit) // width))
        for n in range(fold_rows)
    ]
    r = lax.broadcasted_iota(jnp.int32, (width, sel.shape[2]), 0)
    s = lax.broadcasted_iota(jnp.int32, (width, sel.shape[2]), 1)
    for o in range(band):
        length = sizes[atom(o - 1)]
        if o != 1:
            length = jnp.where(screen[o, atom(0)] == 1, length, 0)
        for i, (_, lane, span) in enumerate(spots):
            sel[i, o * width : (o + 1) * width, : span * width] = jnp.where(
                (s - r == at + lane) & (r < length), 1.0, 0.0
            ).astype(sel.dtype)[:, : span * width]
        at = at + length

    def fold(values):
        folded = [None] * tiles
        for (start, _, span), v in zip(spots, values):
            for n in range(span):
                piece = v[:, n * width : (n + 1) * width]
                before = folded[start + n]
                folded[start + n] = piece if before is None else before + piece
        return folded

    def pack(part):
        slot = lax.rem(part, 2)
        own_copy(part).wait()

        @pl.when(part + 1 < parts)
        def _():
            own_copy(part + 1).start()

        def some(g, carry):
            x = own[slot, pl.ds(g * 4 * rows, 4 * rows)]
            x = x.reshape(4 * units, fold_rows, band, ROWS, width)
            values = [
                mm(
                    jnp.concatenate(
                        [x[:, i, n].reshape(4 * units * ROWS, width) for n in range(band)], axis=1
                    ),
                    sel[i, :, : spots[i][2] * width],
                )
                for i in range(fold_rows)
            ]
            for t, v in enumerate(fold(values)):
                msend[part, pl.ds(g * 4, 4), :, t] = v.astype(jnp.bfloat16).reshape(
                    4, units, ROWS, width
                )
            return carry

        lax.fori_loop(0, nblk // 4, some, 0)

    pack(jnp.int32(0))
    pl.semaphore_wait(barrier, len(PLANE) + nctr - 1)

    for slot, shift in ((0, 1), (1, -1)):
        send(
            gv_hbm, gvn.at[2 * slot], gv_sems.at[0, slot], gv_sems.at[1, slot], blk, atom(shift)
        )

    def first_sends(part, carry):
        piece = pl.ds(part * ROWS, ROWS)
        for slot, shift in ((0, 1), (1, -1)):
            send(
                tc.at[:, :, piece, :], halo.at[slot, part],
                halo_sems.at[0, slot, part], halo_sems.at[1, slot, part], blk, atom(shift),
            )

        @pl.when(part > 0)
        def _():
            pack(part)

        for cut in range(2):
            some = pl.ds(cut * (units // 2), units // 2)
            for dy, dz in PLANE:
                b = peer(dy, dz)
                send(
                    msend.at[part, b, some], mrecv.at[blk, some, :, piece, :],
                    m_sems.at[0], m_sems.at[1], b, ctr,
                )
        pltpu.make_async_copy(
            msend.at[part, blk], mrecv.at[blk, :, :, piece, :], slot_sem
        ).start()
        return carry

    lax.fori_loop(0, parts, first_sends, 0)
    own_copy(0).start()

    wide = 2 * band - 1
    terms = [(e, j) for e in range(wide) for j in range(band) if 0 <= e - j < band]
    r = lax.broadcasted_iota(jnp.int32, (width, width), 0)
    s = lax.broadcasted_iota(jnp.int32, (width, width), 1)
    for copy in inputs:
        copy.wait()
    height = width // fold_rows
    place = fold_rows * r
    for n in range(1, fold_rows):
        place = place - jnp.where(r >= n * height, width - 1, 0)
    order = jnp.where(s == place, 1.0, 0.0).astype(jnp.bfloat16)
    for n, (e, j) in enumerate(terms):
        k = e - j
        keep = (r < sizes[atom(0)]) & (s < sizes[atom(j - 1)])
        if k != 1:
            keep = keep & (screen[k, atom(j - 1)] == 1)
        block = jnp.where(keep, go[j], jnp.zeros_like(go[j]))
        gomat[:, n * width : (n + 1) * width] = mm(order, block).astype(gomat.dtype)
    for slot in range(2):
        wait(gvn.at[2 * slot], gv_sems.at[1, slot])

    for e in range(wide):
        for o in range(band):
            here = (pl.ds(e * width, width), pl.ds(o * width, width))
            if not 0 <= e - o < band:
                gmat[here] = jnp.zeros((width, width), gmat.dtype)
                continue
            keep = (r < sizes[atom(e - 2)]) & (s < sizes[atom(o - 1)])
            if o != 1:
                keep = keep & (screen[o, atom(0)] == 1)
            gmat[here] = jnp.where(keep, gvn[o, e - o], jnp.zeros((width, width), gmat.dtype))

    def second_sends(part):
        for cut in range(2):
            some = pl.ds(cut * (units // 2), units // 2)
            for dy, dz in PLANE:
                b = peer(dy, dz)
                send(
                    bsend.at[part, b, some], brecv.at[part, blk, some],
                    b_send_sem, b_recv_sem.at[part], b, ctr,
                )
        pltpu.make_async_copy(bsend.at[part, blk], brecv.at[part, blk], b_own_sem.at[part]).start()

    for i, (_, _, span) in enumerate(spots):
        pgmat[i, :, : span * width] = mm(gmat[...], sel[i, :, : span * width]).astype(pgmat.dtype)

    def transform(part, carry):
        slot = lax.rem(part, 2)
        own_copy(part).wait()

        @pl.when(part + 1 < parts)
        def _():
            own_copy(part + 1).start()

        step = 16
        for j in (1, 0, 2):
            if j != 1:
                wait(halo.at[j // 2, part], halo_sems.at[1, j // 2, part])

            def columns(t, carry):
                at = pl.ds(t * step, step)
                x = own[slot, at] if j == 1 else halo[j // 2, part, at]
                for k in range(band):
                    y = x[:, k].reshape(step * ROWS, width).astype(jnp.float32)
                    ms[j, k, pl.ds(t * step * ROWS, step * ROWS), :] = y
                return carry

            lax.fori_loop(0, width // step, columns, 0)

        def green(g, carry):
            places = [pl.ds(g * AT_ONCE + p, width, stride=ROWS) for p in range(AT_ONCE)]
            half = []
            for e in range(wide):
                js = [n for n, (of, _) in enumerate(terms) if of == e]
                right = jnp.concatenate(
                    [
                        jnp.concatenate(
                            [
                                ms[terms[n][1], e - terms[n][1], at, :].astype(jnp.bfloat16)
                                for at in places
                            ],
                            axis=1,
                        )
                        for n in js
                    ],
                    axis=0,
                )
                left = gomat[:, js[0] * width : (js[-1] + 1) * width]
                half.append(mm(left, right).astype(jnp.bfloat16))
            both = []
            for i in range(fold_rows):
                left = jnp.concatenate(
                    [
                        jnp.concatenate(
                            [
                                h[
                                    i * height : (i + 1) * height,
                                    p * width : (p + 1) * width,
                                ]
                                for h in half
                            ],
                            axis=1,
                        )
                        for p in range(AT_ONCE)
                    ],
                    axis=0,
                )
                both.append(mm(left, pgmat[i, :, : spots[i][2] * width]))
            for t, v in enumerate(fold(both)):
                for p in range(AT_ONCE):
                    at = pl.ds(g * AT_ONCE + p, height, stride=ROWS)
                    bsc[t, at, :] = v[p * height : (p + 1) * height]
            return carry

        lax.fori_loop(0, ROWS // AT_ONCE, green, 0)

        def rounded(i, carry):
            for t in range(tiles):
                b = bsc[t, pl.ds(i * units * ROWS, units * ROWS), :].astype(jnp.bfloat16)
                bsend[part, i, :, t] = b.reshape(units, ROWS, width)
            return carry

        lax.fori_loop(0, nblk, rounded, 0)

        @pl.when(part > 0)
        def _():
            second_sends(part - 1)

        return carry

    lax.fori_loop(0, parts, transform, 0)

    wait(mrecv.at[blk], slot_sem)
    wait(mrecv.at[pl.ds(0, nblk - 1)], m_sems.at[1])

    group = nblk // TILES
    cols = nblk * ROWS
    last = parts - 1

    def first(t):
        return lax.rem(y + t, TILES) * group

    def product(part, sent, got, send_sem):
        pltpu.make_async_copy(bsend.at[part, blk], brecv.at[part, blk], b_own_sem.at[part]).wait()
        wait(brecv.at[part, pl.ds(0, nblk - 1)], b_recv_sem.at[part])

        def tile(t, carry):
            at = pl.ds(first(t), group)
            here = pl.ds(pl.multiple_of(t * group * 8, group * 8), group * 8)
            acc = None
            step = 4 // fold_rows
            for m0 in range(0, units, step):
                pairs = [(m, o) for m in range(m0, m0 + step) for o in range(tiles)]
                left = jnp.concatenate(
                    [mrecv[at, m, o].reshape(group * share, width) for m, o in pairs], axis=1
                )
                right = jnp.concatenate(
                    [brecv[part, :, m, o].reshape(cols, width) for m, o in pairs], axis=1
                )
                term = mm_nt(left, right)
                acc = term if acc is None else acc + term
            acc = acc.reshape(group, nctr, 8, cols)
            for c in range(nctr):
                sent[c, here, :] = acc[:, c].reshape(group * 8, cols).astype(sent.dtype)
            for d in range(1, nctr):
                c = atom(d)
                send(
                    sent.at[c, here, :], got.at[d - 1, here, :],
                    send_sem, x_recv_sem.at[part, t], blk, c,
                )
            return carry

        lax.fori_loop(0, TILES, tile, 0)

    def reduce(part, sent, got):
        def tile(t, carry):
            here = pl.ds(pl.multiple_of(t * group * 8, group * 8), group * 8)
            wait(got.at[:, here, :], x_recv_sem.at[part, t])
            total = sent[ctr, here, :].astype(jnp.float32)
            for d in range(nctr - 1):
                total = total + got[d, here, :].astype(jnp.float32)
            ysend[part, here, :] = total
            for i in range(group):
                b = first(t) + i
                row = pl.ds(pl.multiple_of((t * group + i) * 8, 8), 8)

                @pl.when(b == blk)
                def _():
                    yrecv[part, blk] = ysend[part, row, :]

                @pl.when(b != blk)
                def _():
                    send(ysend.at[part, row, :], yrecv.at[part, blk], y_send_sem, y_recv_sem, b, ctr)

            return carry

        lax.fori_loop(0, TILES, tile, 0)

    def middle(part, carry):
        product(part, xsend.at[part], xrecv.at[part], x_send_sems.at[0])

        @pl.when(part == 1)
        def _():
            second_sends(last)

        @pl.when(part > 0)
        def _():
            reduce(part - 1, xsend.at[part - 1], xrecv.at[part - 1])

        return carry

    lax.fori_loop(0, last, middle, 0)
    product(last, xsend_last, xrecv_last, x_send_sems.at[1])
    reduce(last - 1, xsend.at[last - 1], xrecv.at[last - 1])
    reduce(last, xsend_last, xrecv_last)

    scale = -2.0 / (width * math.sqrt(nctr * band))
    wait(yrecv.at[:, pl.ds(0, nblk - 1)], y_recv_sem)
    lane = lax.broadcasted_iota(jnp.int32, (8, LANES), 1)
    held = [jnp.zeros((8, LANES), jnp.float32) for _ in range(nblk * share // LANES)]
    for part in range(parts):
        total = yrecv[part, 0]
        for n in range(1, nblk):
            total = total + yrecv[part, n]
        total = total * scale
        for n in range(nblk):
            at, to = n * ROWS, n * share + part * ROWS
            piece = total[:, at // LANES * LANES : (at // LANES + 1) * LANES]
            shift = (to - at) % LANES
            if shift:
                piece = pltpu.roll(piece, shift, 1)
            here = (lane >= to % LANES) & (lane < to % LANES + ROWS)
            held[to // LANES] = jnp.where(here, piece, held[to // LANES])
    for n, piece in enumerate(held):
        out[:, n * LANES : (n + 1) * LANES] = piece

    for slot in range(2):
        wait(gvn.at[2 * slot], gv_sems.at[0, slot])
        for part in range(parts):
            wait(halo.at[slot, part], halo_sems.at[0, slot, part])
    wait(mrecv.at[pl.ds(0, nblk - 1)], m_sems.at[0])
    wait(brecv.at[:, pl.ds(0, nblk - 1)], b_send_sem)
    wait(xrecv, x_send_sems.at[0])
    wait(xrecv_last, x_send_sems.at[1])
    wait(yrecv.at[:, pl.ds(0, nblk - 1)], y_send_sem)


def run(fold_rows, three_centre, green_occupied, green_virtual, block_sizes, screening):
    _, width, band, share, _ = three_centre.shape
    nblk, nctr = lax.axis_size("blk"), lax.axis_size("ctr")
    parts, rows, cols = share // ROWS, width // nblk, nblk * ROWS
    bf16, f32 = jnp.bfloat16, jnp.float32
    vmem, dma = pltpu.VMEM, pltpu.SemaphoreType.DMA
    packed = fold_rows > 1
    units, tiles = rows // fold_rows, FOLDS[fold_rows]
    early = bf16 if fold_rows > 2 else f32
    reach = (fold_rows // 2 + 2) * width
    one = lambda *a: [vmem(*a)] if packed else []
    return pl.pallas_call(
        functools.partial(packed_kernel, fold_rows) if packed else kernel,
        out_shape=jax.ShapeDtypeStruct((8, nblk * share), f32),
        in_specs=[
            pl.BlockSpec(memory_space=pl.ANY),
            pl.BlockSpec(memory_space=pl.ANY),
            pl.BlockSpec(memory_space=pl.ANY),
            pl.BlockSpec(memory_space=pltpu.SMEM),
            pl.BlockSpec(memory_space=pltpu.SMEM),
        ],
        out_specs=pl.BlockSpec(memory_space=pltpu.VMEM),
        scratch_shapes=[
            vmem((2, width, band, ROWS, width), bf16),
            vmem((2, parts, width, band, ROWS, width), bf16),
            *one((parts, nblk, units, tiles, ROWS, width), bf16),
            vmem((nblk, units, tiles, share, width), bf16),
            vmem((parts, nblk, units, tiles, ROWS, width), bf16),
            vmem((parts, nblk, units, tiles, ROWS, width), bf16),
            vmem((band, width, width), bf16),
            vmem((3, band, width, width), bf16),
            vmem(((2 * band - 1) * width, band * width), bf16),
            vmem((width, band * band * width), bf16),
            *one((fold_rows, band * width, reach), bf16),
            *one((fold_rows, (2 * band - 1) * width, reach), bf16),
            vmem((band, band, width * ROWS, width), f32),
            vmem((tiles, width * ROWS * units // rows, width), f32),
            vmem((parts - 1, nctr, nblk * 8, cols), early),
            vmem((parts - 1, nctr - 1, nblk * 8, cols), early),
            vmem((nctr, nblk * 8, cols), bf16),
            vmem((nctr - 1, nblk * 8, cols), bf16),
            vmem((parts, nblk * 8, cols), f32),
            vmem((parts, nblk, 8, cols), f32),
            dma((2,)),
            dma((2,)),
            dma,
            dma((2, 2)),
            dma((2, 2, parts)),
            dma((2,)),
            dma,
            dma((parts,)),
            dma((parts,)),
            dma((2,)),
            dma((parts, TILES)),
            dma,
            dma,
        ],
        compiler_params=pltpu.CompilerParams(
            collective_id=list(FOLDS).index(fold_rows), has_side_effects=True, vmem_limit_bytes=62 << 20
        ),
        name="response_%d" % fold_rows,
    )(three_centre[0], green_occupied[0], green_virtual[0], block_sizes, screening.T)


def per_device(*args):
    sizes, screen = args[3], args[4]
    band = screen.shape[1]
    cols = pl.pallas_call(
        most_columns,
        out_shape=jax.ShapeDtypeStruct((1,), jnp.int32),
        in_specs=[pl.BlockSpec(memory_space=pltpu.SMEM)] * 2,
        out_specs=pl.BlockSpec(memory_space=pltpu.SMEM),
        name="most_columns",
    )(sizes, screen.T)
    width = args[0].shape[1]
    limits = {f: t * width // f for f, t in FOLDS.items() if f > 1}
    branch = sum((cols[0] > limit).astype(jnp.int32) for limit in limits.values())
    return lax.switch(branch, [functools.partial(run, f) for f in (*limits, 1)], *args)


def solution(mesh):
    return jax.shard_map(
        per_device,
        mesh=mesh,
        in_specs=(
            P("ctr", None, None, "blk", None),
            P("ctr", None, None, None),
            P("ctr", None, None, None),
            P(),
            P(),
        ),
        out_specs=P(("blk", "ctr"), None),
        check_vma=False,
    )
```

```python
import functools
import math

import jax
import jax.numpy as jnp
from jax import lax
from jax.experimental import pallas as pl
from jax.experimental.pallas import tpu as pltpu
from jax.sharding import PartitionSpec as P

MESH = pl.DeviceIdType.MESH
SIDE = 4
ROWS = 16
TILES = 4
LANES = 128
FOLDS = {2: 5, 4: 11, 1: 3}
AT_ONCE = 4

PLANE = (
    (2, 2), (1, 2), (3, 2), (2, 1), (2, 3),
    (0, 2), (2, 0), (1, 1), (3, 3), (1, 3), (3, 1),
    (0, 1), (0, 3), (1, 0), (3, 0),
)


def mm(a, b):
    return jnp.dot(a, b, preferred_element_type=jnp.float32)


def mm_nt(a, b):
    return lax.dot_general(a, b, (((1,), (1,)), ((), ())), preferred_element_type=jnp.float32)


def kernel(
    tc, go_hbm, gv_hbm, sizes, screen, out,
    own, halo, mrecv, bsend, brecv, go, gvn, gmat, gomat, ms, bsc,
    xsend, xrecv, xsend_last, xrecv_last, ysend, yrecv,
    in_sems, own_sem, slot_sem, gv_sems, halo_sems, m_sems, b_send_sem, b_recv_sem, b_own_sem,
    x_send_sems, x_recv_sem, y_send_sem, y_recv_sem,
):
    width, band, share, _ = tc.shape
    parts = share // ROWS
    nblk = mrecv.shape[0]
    nctr = lax.axis_size("ctr")
    rows = width // nblk
    blk, ctr = lax.axis_index("blk"), lax.axis_index("ctr")
    y, z = blk // SIDE, lax.rem(blk, SIDE)

    def peer(dy, dz):
        return lax.rem(y + dy, SIDE) * SIDE + lax.rem(z + dz, SIDE)

    def atom(shift):
        return lax.rem(ctr + shift + nctr, nctr)

    def send(src, dst, send_sem, recv_sem, b, c):
        pltpu.make_async_remote_copy(
            src_ref=src, dst_ref=dst, send_sem=send_sem, recv_sem=recv_sem,
            device_id=(b, c), device_id_type=MESH,
        ).start()

    def wait(ref, sem):
        pltpu.make_async_copy(ref, ref, sem).wait()

    def own_copy(part):
        slot = lax.rem(part, 2)
        return pltpu.make_async_copy(
            tc.at[:, :, pl.ds(part * ROWS, ROWS), :], own.at[slot], own_sem.at[slot]
        )

    inputs = [
        pltpu.make_async_copy(src, dst, in_sems.at[n])
        for n, (src, dst) in enumerate(
            ((go_hbm, go), (gv_hbm, gvn.at[1]))
        )
    ]
    for copy in inputs:
        copy.start()
    own_copy(0).start()
    slot_copy = pltpu.make_async_copy(tc.at[pl.ds(blk * rows, rows)], mrecv.at[blk], slot_sem)
    slot_copy.start()

    barrier = pltpu.get_barrier_semaphore()
    for dy, dz in PLANE:
        pl.semaphore_signal(barrier, inc=1, device_id=(peer(dy, dz), ctr), device_id_type=MESH)
    for d in range(1, nctr):
        pl.semaphore_signal(barrier, inc=1, device_id=(blk, atom(d)), device_id_type=MESH)
    pl.semaphore_wait(barrier, len(PLANE) + nctr - 1)

    for slot, shift in ((0, 1), (1, -1)):
        send(
            gv_hbm, gvn.at[2 * slot], gv_sems.at[0, slot], gv_sems.at[1, slot], blk, atom(shift)
        )

    def first_sends(part, carry):
        piece = pl.ds(part * ROWS, ROWS)
        for slot, shift in ((0, 1), (1, -1)):
            send(
                tc.at[:, :, piece, :], halo.at[slot, part],
                halo_sems.at[0, slot, part], halo_sems.at[1, slot, part], blk, atom(shift),
            )
        for cut in range(2):
            some = rows // 2
            for dy, dz in PLANE:
                b = peer(dy, dz)
                send(
                    tc.at[pl.ds(b * rows + cut * some, some), :, piece, :],
                    mrecv.at[blk, pl.ds(cut * some, some), :, piece, :],
                    m_sems.at[0], m_sems.at[1], b, ctr,
                )
        return carry

    lax.fori_loop(0, parts, first_sends, 0)

    wide = 2 * band - 1
    terms = [(e, j) for e in range(wide) for j in range(band) if 0 <= e - j < band]
    r = lax.broadcasted_iota(jnp.int32, (width, width), 0)
    s = lax.broadcasted_iota(jnp.int32, (width, width), 1)
    for copy in inputs:
        copy.wait()
    for n, (e, j) in enumerate(terms):
        k = e - j
        keep = (r < sizes[atom(0)]) & (s < sizes[atom(j - 1)])
        if k != 1:
            keep = keep & (screen[k, atom(j - 1)] == 1)
        gomat[:, n * width : (n + 1) * width] = jnp.where(keep, go[j], jnp.zeros_like(go[j]))
    for slot in range(2):
        wait(gvn.at[2 * slot], gv_sems.at[1, slot])

    for e in range(wide):
        for o in range(band):
            here = (pl.ds(e * width, width), pl.ds(o * width, width))
            if not 0 <= e - o < band:
                gmat[here] = jnp.zeros((width, width), gmat.dtype)
                continue
            keep = (r < sizes[atom(e - 2)]) & (s < sizes[atom(o - 1)])
            if o != 1:
                keep = keep & (screen[o, atom(0)] == 1)
            gmat[here] = jnp.where(keep, gvn[o, e - o], jnp.zeros((width, width), gmat.dtype))

    def second_sends(part):
        for cut in range(2):
            some = pl.ds(cut * (rows // 2), rows // 2)
            for dy, dz in PLANE:
                b = peer(dy, dz)
                send(
                    bsend.at[part, b, some], brecv.at[part, blk, some],
                    b_send_sem, b_recv_sem.at[part], b, ctr,
                )
        pltpu.make_async_copy(bsend.at[part, blk], brecv.at[part, blk], b_own_sem.at[part]).start()

    def transform(part, carry):
        slot = lax.rem(part, 2)
        own_copy(part).wait()

        @pl.when(part + 1 < parts)
        def _():
            own_copy(part + 1).start()

        step = 16
        for j in (1, 0, 2):
            if j != 1:
                wait(halo.at[j // 2, part], halo_sems.at[1, j // 2, part])

            def columns(t, carry):
                at = pl.ds(t * step, step)
                x = own[slot, at] if j == 1 else halo[j // 2, part, at]
                for k in range(band):
                    y = x[:, k].reshape(step * ROWS, width).astype(jnp.float32)
                    ms[j, k, pl.ds(t * step * ROWS, step * ROWS), :] = y
                return carry

            lax.fori_loop(0, width // step, columns, 0)

        def green(g, carry):
            places = [pl.ds(g * AT_ONCE + p, width, stride=ROWS) for p in range(AT_ONCE)]
            half = []
            for e in range(wide):
                js = [n for n, (of, _) in enumerate(terms) if of == e]
                right = jnp.concatenate(
                    [
                        jnp.concatenate(
                            [
                                ms[terms[n][1], e - terms[n][1], at, :].astype(jnp.bfloat16)
                                for at in places
                            ],
                            axis=1,
                        )
                        for n in js
                    ],
                    axis=0,
                )
                left = gomat[:, js[0] * width : (js[-1] + 1) * width]
                half.append(mm(left, right).astype(jnp.bfloat16))
            left = jnp.concatenate(
                [
                    jnp.concatenate([h[:, p * width : (p + 1) * width] for h in half], axis=1)
                    for p in range(AT_ONCE)
                ],
                axis=0,
            )
            b = mm(left, gmat[...])
            for p, at in enumerate(places):
                for o in range(band):
                    bsc[o, at, :] = b[p * width : (p + 1) * width, o * width : (o + 1) * width]
            return carry

        lax.fori_loop(0, ROWS // AT_ONCE, green, 0)

        def rounded(i, carry):
            for o in range(band):
                b = bsc[o, pl.ds(i * rows * ROWS, rows * ROWS), :].astype(jnp.bfloat16)
                bsend[part, i, :, o] = b.reshape(rows, ROWS, width)
            return carry

        lax.fori_loop(0, nblk, rounded, 0)

        @pl.when(part > 0)
        def _():
            second_sends(part - 1)

        return carry

    lax.fori_loop(0, parts, transform, 0)

    slot_copy.wait()
    wait(mrecv.at[pl.ds(0, nblk - 1)], m_sems.at[1])

    group = nblk // TILES
    cols = nblk * ROWS
    last = parts - 1

    def first(t):
        return lax.rem(y + t, TILES) * group

    def product(part, sent, got, send_sem):
        pltpu.make_async_copy(bsend.at[part, blk], brecv.at[part, blk], b_own_sem.at[part]).wait()
        wait(brecv.at[part, pl.ds(0, nblk - 1)], b_recv_sem.at[part])

        def tile(t, carry):
            at = pl.ds(first(t), group)
            here = pl.ds(pl.multiple_of(t * group * 8, group * 8), group * 8)
            acc = None
            for m0 in range(0, rows, 2):
                pairs = [(m, o) for m in (m0, m0 + 1) for o in range(band)]
                left = jnp.concatenate(
                    [mrecv[at, m, o].reshape(group * share, width) for m, o in pairs], axis=1
                )
                right = jnp.concatenate(
                    [brecv[part, :, m, o].reshape(cols, width) for m, o in pairs], axis=1
                )
                term = mm_nt(left, right)
                acc = term if acc is None else acc + term
            acc = acc.reshape(group, nctr, 8, cols)
            for c in range(nctr):
                sent[c, here, :] = acc[:, c].reshape(group * 8, cols).astype(sent.dtype)
            for d in range(1, nctr):
                c = atom(d)
                send(
                    sent.at[c, here, :], got.at[d - 1, here, :],
                    send_sem, x_recv_sem.at[part, t], blk, c,
                )
            return carry

        lax.fori_loop(0, TILES, tile, 0)

    def reduce(part, sent, got):
        def tile(t, carry):
            here = pl.ds(pl.multiple_of(t * group * 8, group * 8), group * 8)
            wait(got.at[:, here, :], x_recv_sem.at[part, t])
            total = sent[ctr, here, :].astype(jnp.float32)
            for d in range(nctr - 1):
                total = total + got[d, here, :].astype(jnp.float32)
            ysend[part, here, :] = total
            for i in range(group):
                b = first(t) + i
                row = pl.ds(pl.multiple_of((t * group + i) * 8, 8), 8)

                @pl.when(b == blk)
                def _():
                    yrecv[part, blk] = ysend[part, row, :]

                @pl.when(b != blk)
                def _():
                    send(ysend.at[part, row, :], yrecv.at[part, blk], y_send_sem, y_recv_sem, b, ctr)

            return carry

        lax.fori_loop(0, TILES, tile, 0)

    def middle(part, carry):
        product(part, xsend.at[part], xrecv.at[part], x_send_sems.at[0])

        @pl.when(part == 1)
        def _():
            second_sends(last)

        @pl.when(part > 0)
        def _():
            reduce(part - 1, xsend.at[part - 1], xrecv.at[part - 1])

        return carry

    lax.fori_loop(0, last, middle, 0)
    product(last, xsend_last, xrecv_last, x_send_sems.at[1])
    reduce(last - 1, xsend.at[last - 1], xrecv.at[last - 1])
    reduce(last, xsend_last, xrecv_last)

    scale = -2.0 / (width * math.sqrt(nctr * band))
    wait(yrecv.at[:, pl.ds(0, nblk - 1)], y_recv_sem)
    lane = lax.broadcasted_iota(jnp.int32, (8, LANES), 1)
    held = [jnp.zeros((8, LANES), jnp.float32) for _ in range(nblk * share // LANES)]
    for part in range(parts):
        total = yrecv[part, 0]
        for n in range(1, nblk):
            total = total + yrecv[part, n]
        total = total * scale
        for n in range(nblk):
            at, to = n * ROWS, n * share + part * ROWS
            piece = total[:, at // LANES * LANES : (at // LANES + 1) * LANES]
            shift = (to - at) % LANES
            if shift:
                piece = pltpu.roll(piece, shift, 1)
            here = (lane >= to % LANES) & (lane < to % LANES + ROWS)
            held[to // LANES] = jnp.where(here, piece, held[to // LANES])
    for n, piece in enumerate(held):
        out[:, n * LANES : (n + 1) * LANES] = piece

    for slot in range(2):
        wait(gvn.at[2 * slot], gv_sems.at[0, slot])
        for part in range(parts):
            wait(halo.at[slot, part], halo_sems.at[0, slot, part])
    wait(mrecv.at[pl.ds(0, nblk - 1)], m_sems.at[0])
    wait(brecv.at[:, pl.ds(0, nblk - 1)], b_send_sem)
    wait(xrecv, x_send_sems.at[0])
    wait(xrecv_last, x_send_sems.at[1])
    wait(yrecv.at[:, pl.ds(0, nblk - 1)], y_send_sem)


def most_columns(sizes, screen, out):
    atoms, band = sizes.shape[0], screen.shape[0]
    most = jnp.int32(0)
    for a in range(atoms):
        total = sizes[a]
        for k in (0, band - 1):
            total = total + jnp.where(screen[k, a] == 1, sizes[(a + k - 1) % atoms], 0)
        most = jnp.maximum(most, total)
    out[0] = most


def packed_kernel(
    fold_rows, tc, go_hbm, gv_hbm, sizes, screen, out,
    own, halo, msend, mrecv, bsend, brecv, go, gvn, gmat, gomat, sel, pgmat, ms, bsc,
    xsend, xrecv, xsend_last, xrecv_last, ysend, yrecv,
    in_sems, own_sem, slot_sem, gv_sems, halo_sems, m_sems, b_send_sem, b_recv_sem, b_own_sem,
    x_send_sems, x_recv_sem, y_send_sem, y_recv_sem,
):
    width, band, share, _ = tc.shape
    parts = share // ROWS
    nblk = mrecv.shape[0]
    nctr = lax.axis_size("ctr")
    rows = width // nblk
    blk, ctr = lax.axis_index("blk"), lax.axis_index("ctr")
    y, z = blk // SIDE, lax.rem(blk, SIDE)

    def peer(dy, dz):
        return lax.rem(y + dy, SIDE) * SIDE + lax.rem(z + dz, SIDE)

    def atom(shift):
        return lax.rem(ctr + shift + nctr, nctr)

    def send(src, dst, send_sem, recv_sem, b, c):
        pltpu.make_async_remote_copy(
            src_ref=src, dst_ref=dst, send_sem=send_sem, recv_sem=recv_sem,
            device_id=(b, c), device_id_type=MESH,
        ).start()

    def wait(ref, sem):
        pltpu.make_async_copy(ref, ref, sem).wait()

    def own_copy(part):
        slot = lax.rem(part, 2)
        return pltpu.make_async_copy(
            tc.at[:, :, pl.ds(part * ROWS, ROWS), :], own.at[slot], own_sem.at[slot]
        )

    inputs = [
        pltpu.make_async_copy(src, dst, in_sems.at[n])
        for n, (src, dst) in enumerate(
            ((go_hbm, go), (gv_hbm, gvn.at[1]))
        )
    ]
    for copy in inputs:
        copy.start()
    own_copy(0).start()
    barrier = pltpu.get_barrier_semaphore()
    for dy, dz in PLANE:
        pl.semaphore_signal(barrier, inc=1, device_id=(peer(dy, dz), ctr), device_id_type=MESH)
    for d in range(1, nctr):
        pl.semaphore_signal(barrier, inc=1, device_id=(blk, atom(d)), device_id_type=MESH)

    at = jnp.int32(0)
    tiles = mrecv.shape[2]
    units = rows // fold_rows
    limit = tiles * width // fold_rows
    spots = [
        (n * limit // width, n * limit % width, -(-(n * limit % width + limit) // width))
        for n in range(fold_rows)
    ]
    r = lax.broadcasted_iota(jnp.int32, (width, sel.shape[2]), 0)
    s = lax.broadcasted_iota(jnp.int32, (width, sel.shape[2]), 1)
    for o in range(band):
        length = sizes[atom(o - 1)]
        if o != 1:
            length = jnp.where(screen[o, atom(0)] == 1, length, 0)
        for i, (_, lane, span) in enumerate(spots):
            sel[i, o * width : (o + 1) * width, : span * width] = jnp.where(
                (s - r == at + lane) & (r < length), 1.0, 0.0
            ).astype(sel.dtype)[:, : span * width]
        at = at + length

    def fold(values):
        folded = [None] * tiles
        for (start, _, span), v in zip(spots, values):
            for n in range(span):
                piece = v[:, n * width : (n + 1) * width]
                before = folded[start + n]
                folded[start + n] = piece if before is None else before + piece
        return folded

    def pack(part):
        slot = lax.rem(part, 2)
        own_copy(part).wait()

        @pl.when(part + 1 < parts)
        def _():
            own_copy(part + 1).start()

        def some(g, carry):
            x = own[slot, pl.ds(g * 4 * rows, 4 * rows)]
            x = x.reshape(4 * units, fold_rows, band, ROWS, width)
            values = [
                mm(
                    jnp.concatenate(
                        [x[:, i, n].reshape(4 * units * ROWS, width) for n in range(band)], axis=1
                    ),
                    sel[i, :, : spots[i][2] * width],
                )
                for i in range(fold_rows)
            ]
            for t, v in enumerate(fold(values)):
                msend[part, pl.ds(g * 4, 4), :, t] = v.astype(jnp.bfloat16).reshape(
                    4, units, ROWS, width
                )
            return carry

        lax.fori_loop(0, nblk // 4, some, 0)

    pack(jnp.int32(0))
    pl.semaphore_wait(barrier, len(PLANE) + nctr - 1)

    for slot, shift in ((0, 1), (1, -1)):
        send(
            gv_hbm, gvn.at[2 * slot], gv_sems.at[0, slot], gv_sems.at[1, slot], blk, atom(shift)
        )

    def first_sends(part, carry):
        piece = pl.ds(part * ROWS, ROWS)
        for slot, shift in ((0, 1), (1, -1)):
            send(
                tc.at[:, :, piece, :], halo.at[slot, part],
                halo_sems.at[0, slot, part], halo_sems.at[1, slot, part], blk, atom(shift),
            )

        @pl.when(part > 0)
        def _():
            pack(part)

        for cut in range(2):
            some = pl.ds(cut * (units // 2), units // 2)
            for dy, dz in PLANE:
                b = peer(dy, dz)
                send(
                    msend.at[part, b, some], mrecv.at[blk, some, :, piece, :],
                    m_sems.at[0], m_sems.at[1], b, ctr,
                )
        pltpu.make_async_copy(
            msend.at[part, blk], mrecv.at[blk, :, :, piece, :], slot_sem
        ).start()
        return carry

    lax.fori_loop(0, parts, first_sends, 0)
    own_copy(0).start()

    wide = 2 * band - 1
    terms = [(e, j) for e in range(wide) for j in range(band) if 0 <= e - j < band]
    r = lax.broadcasted_iota(jnp.int32, (width, width), 0)
    s = lax.broadcasted_iota(jnp.int32, (width, width), 1)
    for copy in inputs:
        copy.wait()
    height = width // fold_rows
    place = fold_rows * r
    for n in range(1, fold_rows):
        place = place - jnp.where(r >= n * height, width - 1, 0)
    order = jnp.where(s == place, 1.0, 0.0).astype(jnp.bfloat16)
    for n, (e, j) in enumerate(terms):
        k = e - j
        keep = (r < sizes[atom(0)]) & (s < sizes[atom(j - 1)])
        if k != 1:
            keep = keep & (screen[k, atom(j - 1)] == 1)
        block = jnp.where(keep, go[j], jnp.zeros_like(go[j]))
        gomat[:, n * width : (n + 1) * width] = mm(order, block).astype(gomat.dtype)
    for slot in range(2):
        wait(gvn.at[2 * slot], gv_sems.at[1, slot])

    for e in range(wide):
        for o in range(band):
            here = (pl.ds(e * width, width), pl.ds(o * width, width))
            if not 0 <= e - o < band:
                gmat[here] = jnp.zeros((width, width), gmat.dtype)
                continue
            keep = (r < sizes[atom(e - 2)]) & (s < sizes[atom(o - 1)])
            if o != 1:
                keep = keep & (screen[o, atom(0)] == 1)
            gmat[here] = jnp.where(keep, gvn[o, e - o], jnp.zeros((width, width), gmat.dtype))

    def second_sends(part):
        for cut in range(2):
            some = pl.ds(cut * (units // 2), units // 2)
            for dy, dz in PLANE:
                b = peer(dy, dz)
                send(
                    bsend.at[part, b, some], brecv.at[part, blk, some],
                    b_send_sem, b_recv_sem.at[part], b, ctr,
                )
        pltpu.make_async_copy(bsend.at[part, blk], brecv.at[part, blk], b_own_sem.at[part]).start()

    for i, (_, _, span) in enumerate(spots):
        pgmat[i, :, : span * width] = mm(gmat[...], sel[i, :, : span * width]).astype(pgmat.dtype)

    def transform(part, carry):
        slot = lax.rem(part, 2)
        own_copy(part).wait()

        @pl.when(part + 1 < parts)
        def _():
            own_copy(part + 1).start()

        step = 16
        for j in (1, 0, 2):
            if j != 1:
                wait(halo.at[j // 2, part], halo_sems.at[1, j // 2, part])

            def columns(t, carry):
                at = pl.ds(t * step, step)
                x = own[slot, at] if j == 1 else halo[j // 2, part, at]
                for k in range(band):
                    y = x[:, k].reshape(step * ROWS, width).astype(jnp.float32)
                    ms[j, k, pl.ds(t * step * ROWS, step * ROWS), :] = y
                return carry

            lax.fori_loop(0, width // step, columns, 0)

        def green(g, carry):
            places = [pl.ds(g * AT_ONCE + p, width, stride=ROWS) for p in range(AT_ONCE)]
            half = []
            for e in range(wide):
                js = [n for n, (of, _) in enumerate(terms) if of == e]
                right = jnp.concatenate(
                    [
                        jnp.concatenate(
                            [
                                ms[terms[n][1], e - terms[n][1], at, :].astype(jnp.bfloat16)
                                for at in places
                            ],
                            axis=1,
                        )
                        for n in js
                    ],
                    axis=0,
                )
                left = gomat[:, js[0] * width : (js[-1] + 1) * width]
                half.append(mm(left, right).astype(jnp.bfloat16))
            both = []
            for i in range(fold_rows):
                left = jnp.concatenate(
                    [
                        jnp.concatenate(
                            [
                                h[
                                    i * height : (i + 1) * height,
                                    p * width : (p + 1) * width,
                                ]
                                for h in half
                            ],
                            axis=1,
                        )
                        for p in range(AT_ONCE)
                    ],
                    axis=0,
                )
                both.append(mm(left, pgmat[i, :, : spots[i][2] * width]))
            for t, v in enumerate(fold(both)):
                for p in range(AT_ONCE):
                    at = pl.ds(g * AT_ONCE + p, height, stride=ROWS)
                    bsc[t, at, :] = v[p * height : (p + 1) * height]
            return carry

        lax.fori_loop(0, ROWS // AT_ONCE, green, 0)

        def rounded(i, carry):
            for t in range(tiles):
                b = bsc[t, pl.ds(i * units * ROWS, units * ROWS), :].astype(jnp.bfloat16)
                bsend[part, i, :, t] = b.reshape(units, ROWS, width)
            return carry

        lax.fori_loop(0, nblk, rounded, 0)

        @pl.when(part > 0)
        def _():
            second_sends(part - 1)

        return carry

    lax.fori_loop(0, parts, transform, 0)

    wait(mrecv.at[blk], slot_sem)
    wait(mrecv.at[pl.ds(0, nblk - 1)], m_sems.at[1])

    group = nblk // TILES
    cols = nblk * ROWS
    last = parts - 1

    def first(t):
        return lax.rem(y + t, TILES) * group

    def product(part, sent, got, send_sem):
        pltpu.make_async_copy(bsend.at[part, blk], brecv.at[part, blk], b_own_sem.at[part]).wait()
        wait(brecv.at[part, pl.ds(0, nblk - 1)], b_recv_sem.at[part])

        def tile(t, carry):
            at = pl.ds(first(t), group)
            here = pl.ds(pl.multiple_of(t * group * 8, group * 8), group * 8)
            acc = None
            step = 4 // fold_rows
            for m0 in range(0, units, step):
                pairs = [(m, o) for m in range(m0, m0 + step) for o in range(tiles)]
                left = jnp.concatenate(
                    [mrecv[at, m, o].reshape(group * share, width) for m, o in pairs], axis=1
                )
                right = jnp.concatenate(
                    [brecv[part, :, m, o].reshape(cols, width) for m, o in pairs], axis=1
                )
                term = mm_nt(left, right)
                acc = term if acc is None else acc + term
            acc = acc.reshape(group, nctr, 8, cols)
            for c in range(nctr):
                sent[c, here, :] = acc[:, c].reshape(group * 8, cols).astype(sent.dtype)
            for d in range(1, nctr):
                c = atom(d)
                send(
                    sent.at[c, here, :], got.at[d - 1, here, :],
                    send_sem, x_recv_sem.at[part, t], blk, c,
                )
            return carry

        lax.fori_loop(0, TILES, tile, 0)

    def reduce(part, sent, got):
        def tile(t, carry):
            here = pl.ds(pl.multiple_of(t * group * 8, group * 8), group * 8)
            wait(got.at[:, here, :], x_recv_sem.at[part, t])
            total = sent[ctr, here, :].astype(jnp.float32)
            for d in range(nctr - 1):
                total = total + got[d, here, :].astype(jnp.float32)
            ysend[part, here, :] = total
            for i in range(group):
                b = first(t) + i
                row = pl.ds(pl.multiple_of((t * group + i) * 8, 8), 8)

                @pl.when(b == blk)
                def _():
                    yrecv[part, blk] = ysend[part, row, :]

                @pl.when(b != blk)
                def _():
                    send(ysend.at[part, row, :], yrecv.at[part, blk], y_send_sem, y_recv_sem, b, ctr)

            return carry

        lax.fori_loop(0, TILES, tile, 0)

    def middle(part, carry):
        product(part, xsend.at[part], xrecv.at[part], x_send_sems.at[0])

        @pl.when(part == 1)
        def _():
            second_sends(last)

        @pl.when(part > 0)
        def _():
            reduce(part - 1, xsend.at[part - 1], xrecv.at[part - 1])

        return carry

    lax.fori_loop(0, last, middle, 0)
    product(last, xsend_last, xrecv_last, x_send_sems.at[1])
    reduce(last - 1, xsend.at[last - 1], xrecv.at[last - 1])
    reduce(last, xsend_last, xrecv_last)

    scale = -2.0 / (width * math.sqrt(nctr * band))
    wait(yrecv.at[:, pl.ds(0, nblk - 1)], y_recv_sem)
    lane = lax.broadcasted_iota(jnp.int32, (8, LANES), 1)
    held = [jnp.zeros((8, LANES), jnp.float32) for _ in range(nblk * share // LANES)]
    for part in range(parts):
        total = yrecv[part, 0]
        for n in range(1, nblk):
            total = total + yrecv[part, n]
        total = total * scale
        for n in range(nblk):
            at, to = n * ROWS, n * share + part * ROWS
            piece = total[:, at // LANES * LANES : (at // LANES + 1) * LANES]
            shift = (to - at) % LANES
            if shift:
                piece = pltpu.roll(piece, shift, 1)
            here = (lane >= to % LANES) & (lane < to % LANES + ROWS)
            held[to // LANES] = jnp.where(here, piece, held[to // LANES])
    for n, piece in enumerate(held):
        out[:, n * LANES : (n + 1) * LANES] = piece

    for slot in range(2):
        wait(gvn.at[2 * slot], gv_sems.at[0, slot])
        for part in range(parts):
            wait(halo.at[slot, part], halo_sems.at[0, slot, part])
    wait(mrecv.at[pl.ds(0, nblk - 1)], m_sems.at[0])
    wait(brecv.at[:, pl.ds(0, nblk - 1)], b_send_sem)
    wait(xrecv, x_send_sems.at[0])
    wait(xrecv_last, x_send_sems.at[1])
    wait(yrecv.at[:, pl.ds(0, nblk - 1)], y_send_sem)


def run(fold_rows, three_centre, green_occupied, green_virtual, block_sizes, screening):
    _, width, band, share, _ = three_centre.shape
    nblk, nctr = lax.axis_size("blk"), lax.axis_size("ctr")
    parts, rows, cols = share // ROWS, width // nblk, nblk * ROWS
    bf16, f32 = jnp.bfloat16, jnp.float32
    vmem, dma = pltpu.VMEM, pltpu.SemaphoreType.DMA
    packed = fold_rows > 1
    units, tiles = rows // fold_rows, FOLDS[fold_rows]
    early = bf16
    reach = (fold_rows // 2 + 2) * width
    one = lambda *a: [vmem(*a)] if packed else []
    return pl.pallas_call(
        functools.partial(packed_kernel, fold_rows) if packed else kernel,
        out_shape=jax.ShapeDtypeStruct((8, nblk * share), f32),
        in_specs=[
            pl.BlockSpec(memory_space=pl.ANY),
            pl.BlockSpec(memory_space=pl.ANY),
            pl.BlockSpec(memory_space=pl.ANY),
            pl.BlockSpec(memory_space=pltpu.SMEM),
            pl.BlockSpec(memory_space=pltpu.SMEM),
        ],
        out_specs=pl.BlockSpec(memory_space=pltpu.VMEM),
        scratch_shapes=[
            vmem((2, width, band, ROWS, width), bf16),
            vmem((2, parts, width, band, ROWS, width), bf16),
            *one((parts, nblk, units, tiles, ROWS, width), bf16),
            vmem((nblk, units, tiles, share, width), bf16),
            vmem((parts, nblk, units, tiles, ROWS, width), bf16),
            vmem((parts, nblk, units, tiles, ROWS, width), bf16),
            vmem((band, width, width), bf16),
            vmem((3, band, width, width), bf16),
            vmem(((2 * band - 1) * width, band * width), bf16),
            vmem((width, band * band * width), bf16),
            *one((fold_rows, band * width, reach), bf16),
            *one((fold_rows, (2 * band - 1) * width, reach), bf16),
            vmem((band, band, width * ROWS, width), f32),
            vmem((tiles, width * ROWS * units // rows, width), f32),
            vmem((parts - 1, nctr, nblk * 8, cols), early),
            vmem((parts - 1, nctr - 1, nblk * 8, cols), early),
            vmem((nctr, nblk * 8, cols), bf16),
            vmem((nctr - 1, nblk * 8, cols), bf16),
            vmem((parts, nblk * 8, cols), f32),
            vmem((parts, nblk, 8, cols), f32),
            dma((2,)),
            dma((2,)),
            dma,
            dma((2, 2)),
            dma((2, 2, parts)),
            dma((2,)),
            dma,
            dma((parts,)),
            dma((parts,)),
            dma((2,)),
            dma((parts, TILES)),
            dma,
            dma,
        ],
        compiler_params=pltpu.CompilerParams(
            collective_id=list(FOLDS).index(fold_rows), has_side_effects=True, vmem_limit_bytes=62 << 20
        ),
        name="response_%d" % fold_rows,
    )(three_centre[0], green_occupied[0], green_virtual[0], block_sizes, screening.T)


def per_device(*args):
    sizes, screen = args[3], args[4]
    band = screen.shape[1]
    cols = pl.pallas_call(
        most_columns,
        out_shape=jax.ShapeDtypeStruct((1,), jnp.int32),
        in_specs=[pl.BlockSpec(memory_space=pltpu.SMEM)] * 2,
        out_specs=pl.BlockSpec(memory_space=pltpu.SMEM),
        name="most_columns",
    )(sizes, screen.T)
    width = args[0].shape[1]
    limits = {f: t * width // f for f, t in FOLDS.items() if f > 1}
    branch = sum((cols[0] > limit).astype(jnp.int32) for limit in limits.values())
    return lax.switch(branch, [functools.partial(run, f) for f in (*limits, 1)], *args)


def solution(mesh):
    return jax.shard_map(
        per_device,
        mesh=mesh,
        in_specs=(
            P("ctr", None, None, "blk", None),
            P("ctr", None, None, None),
            P("ctr", None, None, None),
            P(),
            P(),
        ),
        out_specs=P(("blk", "ctr"), None),
        check_vma=False,
    )
```
